512 devices in a mesh: ctx: 128 (over x, y_lo, z, core), tp: 4 (over y_hi).
Axes of the slice: x: 4, y: 8 (y_hi: 4, y_lo: 2; y = y_hi * 2 + y_lo), z: 8, core: 2. Of those that a mesh axis runs over, the one named last changes fastest.
Arguments:
- queries: bfloat16 [8192, 1792], P('ctx', 'tp'), may hold values from -9 to 9
- keys: bfloat16 [8192, 1792], P('ctx', 'tp'), may hold values from -6 to 6
- values: bfloat16 [8192, 1792], P('ctx', 'tp'), may hold values from -6 to 6
- out_weight: bfloat16 [1792, 3584], P('tp'), may hold values from -0.125 to 0.125
Outputs:
- projected: bfloat16 [8192, 3584], P('ctx', 'tp')
The draws below stay inside these ranges and needn't reach their ends.
All inputs are finite; a program needn't handle non-finite values.
Results may differ from the reference program's by a relative error of at most 0.015.
Values may be sent and summed in bfloat16 or wider, within the bound.
No kernel may reach another device: no remote copies, remote signals or barrier semaphores. Data moves between devices by JAX's collectives and lax.ppermute only.
A program may use at most 128 MiB of HBM per device.

```python
import jax
import jax.numpy as jnp
from jax import lax

HEADS = 16
HEAD_DIM = 112
OUT_COLS = 3584
SEQ = 8192


def draw_queries(key, part):
    key = jax.random.fold_in(key, 11)
    drawn = 1.5 * jax.random.truncated_normal(key, -6.0, 6.0, (SEQ, HEADS * HEAD_DIM), jnp.float32)
    return drawn.astype(jnp.bfloat16)


def draw_keys(key, part):
    key = jax.random.fold_in(key, 23)
    drawn = jax.random.truncated_normal(key, -6.0, 6.0, (SEQ, HEADS * HEAD_DIM), jnp.float32)
    return drawn.astype(jnp.bfloat16)


def block_scale(key, dims, cuts, smallest, top_value):
    loudness, own = 1.0, jax.random.fold_in(key, 6)
    for axis_at, shards_of in cuts:
        steps = jnp.exp(jax.random.uniform(jax.random.fold_in(own, axis_at), (shards_of,), jnp.float32, smallest / len(cuts), top_value / len(cuts)))
        loudness = loudness * jnp.repeat(steps, dims[axis_at] // shards_of).reshape([-1 if axis == axis_at else 1 for axis in range(len(dims))])
    return loudness


def scatter_about(rng, dims, deviation, limit, cuts=(), kind=jnp.bfloat16):
    entries = jax.random.normal(rng, dims, jnp.float32) * deviation
    if len(cuts) > 0:
        entries = block_scale(rng, dims, cuts, -0.22, 0.18) * entries
    return jnp.clip(entries, min=-limit, max=limit).astype(kind)


def setup_inputs(seed: int = 0) -> dict:
    key_list = jax.random.split(jax.random.key(seed), 5)
    queries = draw_queries(jax.random.fold_in(key_list[4], 71), 0)
    keys = draw_keys(jax.random.fold_in(key_list[4], 71), 0)
    values = scatter_about(key_list[2], (SEQ, HEADS * HEAD_DIM), 1.0, 6.0, ((0, 128), (1, 4)))
    out_weight = scatter_about(key_list[3], (HEADS * HEAD_DIM, OUT_COLS), (HEADS * HEAD_DIM) ** -0.5, 0.125, ((0, 4),))
    return dict(queries=queries, keys=keys, values=values, out_weight=out_weight)


def reference(queries, keys, values, out_weight):
    seq_rows = queries.shape[0]
    query_heads = jnp.transpose(queries.reshape(seq_rows, HEADS, HEAD_DIM), (1, 0, 2))
    key_heads = jnp.transpose(keys.reshape(seq_rows, HEADS, HEAD_DIM), (1, 0, 2))
    value_heads = jnp.transpose(values.reshape(seq_rows, HEADS, HEAD_DIM), (1, 0, 2))
    positions = jnp.arange(seq_rows, dtype=jnp.int32)
    causal = positions[:, None] >= positions[None, :]
    score_scale = 1.0 / (HEAD_DIM ** 0.5)

    def one_head(operands):
        query_one, key_one, value_one = operands
        scores = jnp.dot(query_one, key_one.T, preferred_element_type=jnp.float32) * score_scale
        row_max = jnp.max(jnp.where(causal, scores, -jnp.inf), axis=1, keepdims=True)
        raw_weights = jnp.where(causal, jnp.exp(scores - row_max), 0.0)
        totals = jnp.sum(raw_weights, axis=1, keepdims=True)
        weights = raw_weights.astype(jnp.bfloat16)
        return jnp.dot(weights, value_one, preferred_element_type=jnp.float32) / totals

    per_head = lax.map(one_head, (query_heads, key_heads, value_heads))
    attention = jnp.transpose(per_head, (1, 0, 2)).reshape(seq_rows, HEADS * HEAD_DIM).astype(jnp.bfloat16)
    return jnp.dot(attention, out_weight, preferred_element_type=jnp.float32).astype(jnp.bfloat16)
```

```python
import math

import jax
import jax.numpy as jnp
from jax import lax
from jax.experimental import pallas as pl
from jax.experimental.pallas import tpu as pltpu
from jax.sharding import Mesh, PartitionSpec as P

HEAD_DIM = 112
LANES = 128
NEG_FILL = -1e30
NEG_CLAMP = -1e29
AXES = ("x", "yl", "zh", "zl", "core", "tp")
CTX = AXES[:5]
QUERY_AXES = ("x", "yl", "zl", "core")
KEY_AXES = ("x", "zh")
VMEM_LIMIT = 48 * 1024 * 1024
EXP2_SCALE = math.log2(math.e) / HEAD_DIM**0.5


def pack_kernel(copies, x_refs, out_ref):
    for head in range(out_ref.shape[0]):
        parts = []
        for x_ref in x_refs:
            own = x_ref[:, head * HEAD_DIM : (head + 1) * HEAD_DIM]
            parts += [own, jnp.zeros((own.shape[0], LANES - HEAD_DIM), own.dtype)]
        block = jnp.concatenate(parts, axis=1)
        for copy in range(copies):
            out_ref[head, copy] = block


def pack(arrays, heads, copies):
    rows = arrays[0].shape[0]

    def body(*refs):
        pack_kernel(copies, refs[:-1], refs[-1])

    return pl.pallas_call(
        body,
        out_shape=jax.ShapeDtypeStruct(
            (heads, copies, rows, LANES * len(arrays)), arrays[0].dtype
        ),
        compiler_params=pltpu.CompilerParams(vmem_limit_bytes=VMEM_LIMIT),
    )(*arrays)


def attend_kernel(x_size, rows, q_ref, kv_ref, out_ref):
    yl, zh, zl, core = (lax.axis_index(name) for name in ("yl", "zh", "zl", "core"))
    block = 4 * rows
    key_count = 4 * rows
    delta = zh * 4 * rows - yl * 16 * rows - zl * 2 * rows - core * rows
    query_at = lax.broadcasted_iota(jnp.int32, (block, key_count), 0)
    key_at = lax.broadcasted_iota(jnp.int32, (block, key_count), 1)
    key_at = (key_at // rows) * (4 * rows) + key_at % rows
    distance = query_at - key_at + delta
    lane = lax.broadcasted_iota(jnp.int32, (block, LANES), 1)
    for x_at in range(x_size):
        known = x_at * key_count
        total = known + key_count
        keys = kv_ref[:total, :LANES]
        values = kv_ref[:total, LANES:]
        lane_v = lax.broadcasted_iota(jnp.int32, (total, LANES), 1)
        values = jnp.where(lane_v == HEAD_DIM, jnp.ones_like(values), values)
        for yl_at in range(2):
            start = (x_at * 2 + yl_at) * block
            queries = q_ref[start : start + block, :]
            scores = lax.dot_general(
                queries, keys, (((1,), (1,)), ((), ())), preferred_element_type=jnp.float32
            )
            last = jnp.where(distance + yl_at * 16 * rows >= 0, scores[:, known:], NEG_FILL)
            if known:
                scores = jnp.concatenate([scores[:, :known], last], axis=1)
            else:
                scores = last
            top = jnp.maximum(jnp.max(scores, axis=1, keepdims=True), NEG_CLAMP)
            weights = jnp.exp2((scores - top) * EXP2_SCALE)
            weighted = jnp.dot(
                weights.astype(jnp.bfloat16), values, preferred_element_type=jnp.float32
            )
            row_total = weighted[:, HEAD_DIM : HEAD_DIM + 1]
            some = row_total > 0.0
            safe = jnp.where(some, row_total, 1.0)
            level = jnp.where(some, top * EXP2_SCALE + jnp.log2(safe), NEG_FILL)
            high = level.astype(jnp.bfloat16).astype(jnp.float32)
            rest = level - high
            middle = rest.astype(jnp.bfloat16).astype(jnp.float32)
            low = rest - middle
            result = weighted * (1.0 / safe)
            result = jnp.where(lane < HEAD_DIM, result, 0.0)
            result = jnp.where(lane == HEAD_DIM, high, result)
            result = jnp.where(lane == HEAD_DIM + 1, middle, result)
            result = jnp.where(lane == HEAD_DIM + 2, low, result)
            out_ref[start : start + block, :] = result.astype(out_ref.dtype)


def attend(queries, keys_values, x_size, rows):
    def body(q_ref, kv_ref, out_ref):
        attend_kernel(x_size, rows, q_ref, kv_ref, out_ref)

    return pl.pallas_call(
        body,
        out_shape=jax.ShapeDtypeStruct(queries.shape, queries.dtype),
        compiler_params=pltpu.CompilerParams(vmem_limit_bytes=VMEM_LIMIT),
    )(queries, keys_values)


def project_kernel(heads, groups, rows, parts_ref, weight_ref, out_ref, attention_ref):
    @pl.when(pl.program_id(0) == 0)
    def _():
        for head in range(heads):
            levels = []
            blocks = []
            for group in range(groups):
                start = (head * groups + group) * rows
                part = parts_ref[start : start + rows, :].astype(jnp.float32)
                blocks.append(part)
                levels.append(
                    part[:, HEAD_DIM : HEAD_DIM + 1]
                    + part[:, HEAD_DIM + 1 : HEAD_DIM + 2]
                    + part[:, HEAD_DIM + 2 : HEAD_DIM + 3]
                )
            top = levels[0]
            for level in levels[1:]:
                top = jnp.maximum(top, level)
            share_sum = jnp.zeros_like(top)
            mixed = jnp.zeros_like(blocks[0])
            for level, part in zip(levels, blocks):
                share = jnp.exp2(level - top)
                share_sum = share_sum + share
                mixed = mixed + share * part
            mixed = mixed / share_sum
            attention_ref[:, head * HEAD_DIM : (head + 1) * HEAD_DIM] = mixed[
                :, :HEAD_DIM
            ].astype(attention_ref.dtype)

    out_ref[0] = jnp.dot(
        attention_ref[...], weight_ref[...], preferred_element_type=jnp.float32
    ).astype(out_ref.dtype)


def project(parts, out_weight, heads, groups, rows, tp_size):
    features, columns = out_weight.shape
    width = columns // tp_size

    def body(parts_ref, weight_ref, out_ref, attention_ref):
        project_kernel(heads, groups, rows, parts_ref, weight_ref, out_ref, attention_ref)

    return pl.pallas_call(
        body,
        grid=(tp_size,),
        in_specs=[
            pl.BlockSpec(parts.shape, lambda i: (0, 0)),
            pl.BlockSpec((features, width), lambda i: (0, i)),
        ],
        out_specs=pl.BlockSpec((1, rows, width), lambda i: (i, 0, 0)),
        out_shape=jax.ShapeDtypeStruct((tp_size, rows, width), jnp.bfloat16),
        scratch_shapes=[pltpu.VMEM((rows, features), jnp.bfloat16)],
        compiler_params=pltpu.CompilerParams(vmem_limit_bytes=VMEM_LIMIT),
    )(parts, out_weight)


def shards(queries, keys, values, out_weight):
    rows, features = queries.shape
    heads = features // HEAD_DIM
    x_size = lax.axis_size("x")
    key_groups = lax.axis_size("yl") * lax.axis_size("zl") * lax.axis_size("core")
    key_parts = lax.axis_size("zh")
    tp_size = lax.axis_size("tp")

    sent_q = pack([queries], heads, key_groups).reshape(heads * key_groups, rows, LANES)
    sent_kv = pack([keys, values], heads, key_parts).reshape(heads * key_parts, rows, 2 * LANES)
    got_q = lax.all_to_all(sent_q, QUERY_AXES, 0, 0, tiled=True)
    got_kv = lax.all_to_all(sent_kv, KEY_AXES, 0, 0, tiled=True)
    partial = attend(
        got_q.reshape(-1, LANES), got_kv.reshape(-1, 2 * LANES), x_size, rows
    )
    returned = lax.all_to_all(
        partial.reshape(heads * key_groups, rows, LANES), QUERY_AXES, 0, 0, tiled=True
    )
    shares = project(
        returned.reshape(-1, LANES), out_weight, heads, key_groups, rows, tp_size
    )
    arrived = lax.all_to_all(shares, "tp", 0, 0, tiled=True)
    return jnp.sum(arrived.astype(jnp.float32), axis=0).astype(jnp.bfloat16)


def solution(mesh):
    split = Mesh(mesh.devices.reshape(4, 2, 4, 2, 2, 4), AXES)
    placed = (P(CTX, "tp"), P(CTX, "tp"), P(CTX, "tp"), P("tp", None))
    return jax.shard_map(
        shards, mesh=split, in_specs=placed, out_specs=P(CTX, "tp"), check_vma=False
    )
```

```python
import math

import jax
import jax.numpy as jnp
from jax import lax
from jax.experimental import pallas as pl
from jax.experimental.pallas import tpu as pltpu
from jax.sharding import Mesh, PartitionSpec as P

HEAD_DIM = 112
LANES = 128
NEG_FILL = -1e30
NEG_CLAMP = -1e29
AXES = ("x", "yl", "zh", "zl", "core", "tp")
CTX = AXES[:5]
QUERY_AXES = ("x", "zh")
KEY_AXES = ("x", "yl", "zl", "core")
VMEM_LIMIT = 48 * 1024 * 1024
EXP2_SCALE = math.log2(math.e) / HEAD_DIM**0.5


def pack_kernel(rows, held, q_out, kv_out):
    for head in range(q_out.shape[0]):
        columns = slice(head * HEAD_DIM, (head + 1) * HEAD_DIM)
        key, value, query = (
            held[part * rows : (part + 1) * rows, columns] for part in range(3)
        )
        gap = jnp.zeros((rows, LANES - HEAD_DIM), key.dtype)
        pair = jnp.concatenate([key, gap, value, gap], axis=1)
        query = jnp.concatenate([query, gap], axis=1)
        for copy in range(kv_out.shape[1]):
            kv_out[head, copy] = pair
        for copy in range(q_out.shape[1]):
            q_out[head, copy] = query


def pack(queries, keys, values, heads, query_copies, key_copies):
    rows = queries.shape[0]
    kind = queries.dtype

    def body(held, q_out, kv_out):
        pack_kernel(rows, held, q_out, kv_out)

    return pl.pallas_call(
        body,
        out_shape=(
            jax.ShapeDtypeStruct((heads, query_copies, rows, LANES), kind),
            jax.ShapeDtypeStruct((heads, key_copies, rows, 2 * LANES), kind),
        ),
        compiler_params=pltpu.CompilerParams(vmem_limit_bytes=VMEM_LIMIT),
    )(jnp.concatenate([keys, values, queries], axis=0))


def attend_kernel(x_size, rows, q_ref, kv_ref, out_ref):
    yl, zh, zl, core = (lax.axis_index(name) for name in ("yl", "zh", "zl", "core"))
    block = 4 * rows
    coarse = 16 * rows
    key_count = 2 * block
    delta = yl * coarse + zl * 2 * rows + core * rows - zh * block
    query_at = lax.broadcasted_iota(jnp.int32, (block, key_count), 0)
    query_at = (query_at // rows) * block + query_at % rows
    key_at = lax.broadcasted_iota(jnp.int32, (block, key_count), 1)
    key_at = (key_at // block) * coarse + key_at % block
    kept = query_at - key_at + delta >= 0
    lane = lax.broadcasted_iota(jnp.int32, (block, LANES), 1)
    for x_at in range(x_size):
        known = x_at * key_count
        total = known + key_count
        keys = kv_ref[:total, :LANES]
        values = kv_ref[:total, LANES:]
        lane_v = lax.broadcasted_iota(jnp.int32, (total, LANES), 1)
        values = jnp.where(lane_v == HEAD_DIM, jnp.ones_like(values), values)
        for start in (x_at * block,):
            queries = q_ref[start : start + block, :]
            scores = lax.dot_general(
                queries, keys, (((1,), (1,)), ((), ())), preferred_element_type=jnp.float32
            )
            last = jnp.where(kept, scores[:, known:], NEG_FILL)
            if known:
                scores = jnp.concatenate([scores[:, :known], last], axis=1)
            else:
                scores = last
            top = jnp.maximum(jnp.max(scores, axis=1, keepdims=True), NEG_CLAMP)
            weights = jnp.exp2((scores - top) * EXP2_SCALE)
            weighted = jnp.dot(
                weights.astype(jnp.bfloat16), values, preferred_element_type=jnp.float32
            )
            row_total = weighted[:, HEAD_DIM : HEAD_DIM + 1]
            some = row_total > 0.0
            safe = jnp.where(some, row_total, 1.0)
            level = jnp.where(some, top * EXP2_SCALE + jnp.log2(safe), NEG_FILL)
            high = level.astype(jnp.bfloat16).astype(jnp.float32)
            rest = level - high
            middle = rest.astype(jnp.bfloat16).astype(jnp.float32)
            low = rest - middle
            result = weighted * (1.0 / safe)
            result = jnp.where(lane < HEAD_DIM, result, 0.0)
            result = jnp.where(lane == HEAD_DIM, high, result)
            result = jnp.where(lane == HEAD_DIM + 1, middle, result)
            result = jnp.where(lane == HEAD_DIM + 2, low, result)
            out_ref[start : start + block, :] = result.astype(out_ref.dtype)


def attend(queries, keys_values, x_size, rows):
    def body(q_ref, kv_ref, out_ref):
        attend_kernel(x_size, rows, q_ref, kv_ref, out_ref)

    return pl.pallas_call(
        body,
        out_shape=jax.ShapeDtypeStruct(queries.shape, queries.dtype),
        compiler_params=pltpu.CompilerParams(vmem_limit_bytes=VMEM_LIMIT),
    )(queries, keys_values)


def project_kernel(heads, groups, rows, parts_ref, weight_ref, out_ref, attention_ref):
    @pl.when(pl.program_id(0) == 0)
    def _():
        for head in range(heads):
            levels = []
            blocks = []
            for group in range(groups):
                start = (head * groups + group) * rows
                part = parts_ref[start : start + rows, :].astype(jnp.float32)
                blocks.append(part)
                levels.append(
                    part[:, HEAD_DIM : HEAD_DIM + 1]
                    + part[:, HEAD_DIM + 1 : HEAD_DIM + 2]
                    + part[:, HEAD_DIM + 2 : HEAD_DIM + 3]
                )
            top = levels[0]
            for level in levels[1:]:
                top = jnp.maximum(top, level)
            share_sum = jnp.zeros_like(top)
            mixed = jnp.zeros_like(blocks[0])
            for level, part in zip(levels, blocks):
                share = jnp.exp2(level - top)
                share_sum = share_sum + share
                mixed = mixed + share * part
            mixed = mixed / share_sum
            attention_ref[:, head * HEAD_DIM : (head + 1) * HEAD_DIM] = mixed[
                :, :HEAD_DIM
            ].astype(attention_ref.dtype)

    out_ref[0] = jnp.dot(
        attention_ref[...], weight_ref[...], preferred_element_type=jnp.float32
    ).astype(out_ref.dtype)


def project(parts, out_weight, heads, groups, rows, tp_size):
    features, columns = out_weight.shape
    width = columns // tp_size

    def body(parts_ref, weight_ref, out_ref, attention_ref):
        project_kernel(heads, groups, rows, parts_ref, weight_ref, out_ref, attention_ref)

    return pl.pallas_call(
        body,
        grid=(tp_size,),
        in_specs=[
            pl.BlockSpec(parts.shape, lambda i: (0, 0)),
            pl.BlockSpec((features, width), lambda i: (0, i)),
        ],
        out_specs=pl.BlockSpec((1, rows, width), lambda i: (i, 0, 0)),
        out_shape=jax.ShapeDtypeStruct((tp_size, rows, width), jnp.bfloat16),
        scratch_shapes=[pltpu.VMEM((rows, features), jnp.bfloat16)],
        compiler_params=pltpu.CompilerParams(vmem_limit_bytes=VMEM_LIMIT),
    )(parts, out_weight)


def shards(queries, keys, values, out_weight):
    rows, features = queries.shape
    heads = features // HEAD_DIM
    x_size = lax.axis_size("x")
    query_copies = lax.axis_size("zh")
    key_copies = lax.axis_size("yl") * lax.axis_size("zl") * lax.axis_size("core")
    tp_size = lax.axis_size("tp")

    sent_q, sent_kv = pack(queries, keys, values, heads, query_copies, key_copies)
    got_q = lax.all_to_all(
        sent_q.reshape(heads * query_copies, rows, LANES), QUERY_AXES, 0, 0, tiled=True
    )
    got_kv = lax.all_to_all(
        sent_kv.reshape(heads * key_copies, rows, 2 * LANES), KEY_AXES, 0, 0, tiled=True
    )
    partial = attend(
        got_q.reshape(-1, LANES), got_kv.reshape(-1, 2 * LANES), x_size, rows
    )
    returned = lax.all_to_all(
        partial.reshape(heads * query_copies, rows, LANES), QUERY_AXES, 0, 0, tiled=True
    )
    shares = project(
        returned.reshape(-1, LANES), out_weight, heads, query_copies, rows, tp_size
    )
    arrived = lax.all_to_all(shares, "tp", 0, 0, tiled=True)
    return jnp.sum(arrived.astype(jnp.float32), axis=0).astype(jnp.bfloat16)


def solution(mesh):
    split = Mesh(mesh.devices.reshape(4, 2, 4, 2, 2, 4), AXES)
    placed = (P(CTX, "tp"), P(CTX, "tp"), P(CTX, "tp"), P("tp", None))
    return jax.shard_map(
        shards, mesh=split, in_specs=placed, out_specs=P(CTX, "tp"), check_vma=False
    )
```

```python
import math

import jax
import jax.numpy as jnp
from jax import lax
from jax.experimental import pallas as pl
from jax.experimental.pallas import tpu as pltpu
from jax.sharding import Mesh, PartitionSpec as P

HEAD_DIM = 112
LANES = 128
TOTAL, TOTAL_LOW, SHIFT = HEAD_DIM, HEAD_DIM + 1, HEAD_DIM + 2
NEG_FILL = -1e30
NEG_CLAMP = -1e29
AXES = ("x", "yl", "zh", "zl", "core", "tp")
CTX = AXES[:5]
QUERY_AXES = ("x", "yl", "zl", "core")
KEY_AXES = ("x", "zh")
VMEM_LIMIT = 48 * 1024 * 1024
EXP2_SCALE = math.log2(math.e) / HEAD_DIM**0.5


def pack_kernel(rows, held, q_out, kv_out):
    for head in range(q_out.shape[0]):
        columns = slice(head * HEAD_DIM, (head + 1) * HEAD_DIM)
        key, value, query = (
            held[part * rows : (part + 1) * rows, columns] for part in range(3)
        )
        gap = jnp.zeros((rows, LANES - HEAD_DIM), key.dtype)
        pair = jnp.concatenate([key, gap, value, jnp.ones_like(gap)], axis=1)
        query = jnp.concatenate([query, gap], axis=1)
        for copy in range(kv_out.shape[1]):
            kv_out[head, copy] = pair
        for copy in range(q_out.shape[1]):
            q_out[head, copy] = query


def pack(queries, keys, values, heads, query_copies, key_copies):
    rows = queries.shape[0]
    kind = queries.dtype

    def body(held, q_out, kv_out):
        pack_kernel(rows, held, q_out, kv_out)

    return pl.pallas_call(
        body,
        out_shape=(
            jax.ShapeDtypeStruct((heads, query_copies, rows, LANES), kind),
            jax.ShapeDtypeStruct((heads, key_copies, rows, 2 * LANES), kind),
        ),
        compiler_params=pltpu.CompilerParams(vmem_limit_bytes=VMEM_LIMIT),
    )(jnp.concatenate([keys, values, queries], axis=0))


def attend_kernel(x_size, rows, q_ref, kv_ref, out_ref):
    yl, zh, zl, core = (lax.axis_index(name) for name in ("yl", "zh", "zl", "core"))
    block = 4 * rows
    coarse = 16 * rows
    delta = zh * block - yl * coarse - zl * 2 * rows - core * rows
    query_at = lax.broadcasted_iota(jnp.int32, (block, block), 0)
    key_at = lax.broadcasted_iota(jnp.int32, (block, block), 1)
    key_at = (key_at // rows) * block + key_at % rows
    distance = query_at - key_at + delta
    lane = lax.broadcasted_iota(jnp.int32, (block, LANES), 1)
    for x_at in range(x_size):
        known = x_at * block
        total = known + block
        keys = kv_ref[:total, :LANES]
        values = kv_ref[:total, LANES:]
        for yl_at in range(2):
            start = (x_at * 2 + yl_at) * block
            queries = q_ref[start : start + block, :]
            scores = lax.dot_general(
                queries, keys, (((1,), (1,)), ((), ())), preferred_element_type=jnp.float32
            )
            last = jnp.where(distance + yl_at * coarse >= 0, scores[:, known:], NEG_FILL)
            if known:
                scores = jnp.concatenate([scores[:, :known], last], axis=1)
            else:
                scores = last
            top = jnp.maximum(jnp.max(scores, axis=1, keepdims=True), NEG_CLAMP) * EXP2_SCALE
            shift = top.astype(jnp.bfloat16).astype(jnp.float32)
            weights = jnp.exp2(scores * EXP2_SCALE - shift)
            weighted = jnp.dot(
                weights.astype(jnp.bfloat16), values, preferred_element_type=jnp.float32
            )
            rounded = weighted.astype(jnp.bfloat16).astype(jnp.float32)
            weighted = jnp.where(lane == TOTAL_LOW, weighted - rounded, weighted)
            weighted = jnp.where(lane == SHIFT, shift, weighted)
            out_ref[start : start + block, :] = weighted.astype(out_ref.dtype)


def attend(queries, keys_values, x_size, rows):
    def body(q_ref, kv_ref, out_ref):
        attend_kernel(x_size, rows, q_ref, kv_ref, out_ref)

    return pl.pallas_call(
        body,
        out_shape=jax.ShapeDtypeStruct(queries.shape, queries.dtype),
        compiler_params=pltpu.CompilerParams(vmem_limit_bytes=VMEM_LIMIT),
    )(queries, keys_values)


def project_kernel(heads, groups, rows, parts_ref, weight_ref, out_ref, attention_ref):
    @pl.when(pl.program_id(0) == 0)
    def _():
        for head in range(heads):
            parts = [
                parts_ref[
                    (head * groups + group) * rows : (head * groups + group + 1) * rows, :
                ].astype(jnp.float32)
                for group in range(groups)
            ]
            shifts = [part[:, SHIFT : SHIFT + 1] for part in parts]
            top = shifts[0]
            for shift in shifts[1:]:
                top = jnp.maximum(top, shift)
            mixed = jnp.zeros_like(parts[0])
            for shift, part in zip(shifts, parts):
                mixed = mixed + jnp.exp2(shift - top) * part
            row_total = (
                mixed[:, TOTAL : TOTAL + 1] + mixed[:, TOTAL_LOW : TOTAL_LOW + 1]
            )
            attention_ref[:, head * HEAD_DIM : (head + 1) * HEAD_DIM] = (
                mixed[:, :HEAD_DIM] / row_total
            ).astype(attention_ref.dtype)

    out_ref[0] = jnp.dot(
        attention_ref[...], weight_ref[...], preferred_element_type=jnp.float32
    ).astype(out_ref.dtype)


def project(parts, out_weight, heads, groups, rows, tp_size):
    features, columns = out_weight.shape
    width = columns // tp_size

    def body(parts_ref, weight_ref, out_ref, attention_ref):
        project_kernel(heads, groups, rows, parts_ref, weight_ref, out_ref, attention_ref)

    return pl.pallas_call(
        body,
        grid=(tp_size,),
        in_specs=[
            pl.BlockSpec(parts.shape, lambda i: (0, 0)),
            pl.BlockSpec((features, width), lambda i: (0, i)),
        ],
        out_specs=pl.BlockSpec((1, rows, width), lambda i: (i, 0, 0)),
        out_shape=jax.ShapeDtypeStruct((tp_size, rows, width), jnp.bfloat16),
        scratch_shapes=[pltpu.VMEM((rows, features), jnp.bfloat16)],
        compiler_params=pltpu.CompilerParams(vmem_limit_bytes=VMEM_LIMIT),
    )(parts, out_weight)


def shards(queries, keys, values, out_weight):
    rows, features = queries.shape
    heads = features // HEAD_DIM
    x_size = lax.axis_size("x")
    query_copies = lax.axis_size("yl") * lax.axis_size("zl") * lax.axis_size("core")
    key_copies = lax.axis_size("zh")
    tp_size = lax.axis_size("tp")

    sent_q, sent_kv = pack(queries, keys, values, heads, query_copies, key_copies)
    got_q = lax.all_to_all(
        sent_q.reshape(heads * query_copies, rows, LANES), QUERY_AXES, 0, 0, tiled=True
    )
    got_kv = lax.all_to_all(
        sent_kv.reshape(heads * key_copies, rows, 2 * LANES), KEY_AXES, 0, 0, tiled=True
    )
    partial = attend(
        got_q.reshape(-1, LANES), got_kv.reshape(-1, 2 * LANES), x_size, rows
    )
    returned = lax.all_to_all(
        partial.reshape(heads * query_copies, rows, LANES), QUERY_AXES, 0, 0, tiled=True
    )
    shares = project(
        returned.reshape(-1, LANES), out_weight, heads, query_copies, rows, tp_size
    )
    arrived = lax.all_to_all(shares, "tp", 0, 0, tiled=True)
    return jnp.sum(arrived.astype(jnp.float32), axis=0).astype(jnp.bfloat16)


def solution(mesh):
    split = Mesh(mesh.devices.reshape(4, 2, 4, 2, 2, 4), AXES)
    placed = (P(CTX, "tp"), P(CTX, "tp"), P(CTX, "tp"), P("tp", None))
    return jax.shard_map(
        shards, mesh=split, in_specs=placed, out_specs=P(CTX, "tp"), check_vma=False
    )
```

```python
import math

import jax
import jax.numpy as jnp
from jax import lax
from jax.experimental import pallas as pl
from jax.experimental.pallas import tpu as pltpu
from jax.sharding import Mesh, PartitionSpec as P

HEAD_DIM = 112
LANES = 128
TOTAL, TOTAL_LOW, SHIFT = HEAD_DIM, HEAD_DIM + 1, HEAD_DIM + 2
NEG_FILL = -1e30
NEG_CLAMP = -1e29
AXES = ("x", "yl", "zh", "zl", "core", "tp")
CTX = AXES[:5]
QUERY_AXES = ("x", "yl", "zl", "core")
KEY_AXES = ("x", "zh")
VMEM_LIMIT = 48 * 1024 * 1024
EXP2_SCALE = math.log2(math.e) / HEAD_DIM**0.5


def pack_kernel(rows, held, q_out, kv_out):
    for head in range(q_out.shape[0]):
        columns = slice(head * HEAD_DIM, (head + 1) * HEAD_DIM)
        key, value, query = (
            held[part * rows : (part + 1) * rows, columns] for part in range(3)
        )
        gap = jnp.zeros((rows, LANES - HEAD_DIM), key.dtype)
        pair = jnp.concatenate([key, gap, value, jnp.ones_like(gap)], axis=1)
        query = jnp.concatenate([query, gap], axis=1)
        for copy in range(kv_out.shape[1]):
            kv_out[head, copy] = pair
        for copy in range(q_out.shape[1]):
            q_out[head, copy] = query


def pack(queries, keys, values, heads, query_copies, key_copies):
    rows = queries.shape[0]
    kind = queries.dtype

    def body(held, q_out, kv_out):
        pack_kernel(rows, held, q_out, kv_out)

    return pl.pallas_call(
        body,
        out_shape=(
            jax.ShapeDtypeStruct((heads, query_copies, rows, LANES), kind),
            jax.ShapeDtypeStruct((heads, key_copies, rows, 2 * LANES), kind),
        ),
        compiler_params=pltpu.CompilerParams(vmem_limit_bytes=VMEM_LIMIT),
    )(jnp.concatenate([keys, values, queries], axis=0))


def attend_kernel(x_size, rows, q_ref, kv_ref, out_ref):
    yl, zh, zl, core = (lax.axis_index(name) for name in ("yl", "zh", "zl", "core"))
    block = 4 * rows
    coarse = 16 * rows
    delta = zh * block - yl * coarse - zl * 2 * rows - core * rows
    query_at = lax.broadcasted_iota(jnp.int32, (block, block), 0)
    key_at = lax.broadcasted_iota(jnp.int32, (block, block), 1)
    key_at = (key_at // rows) * block + key_at % rows
    distance = query_at - key_at + delta
    lane = lax.broadcasted_iota(jnp.int32, (block, LANES), 1)
    for x_at in range(x_size):
        known = x_at * block
        total = known + block
        keys = kv_ref[:total, :LANES]
        values = kv_ref[:total, LANES:]
        for yl_at in range(2):
            start = (x_at * 2 + yl_at) * block
            queries = q_ref[start : start + block, :]
            scores = lax.dot_general(
                queries, keys, (((1,), (1,)), ((), ())), preferred_element_type=jnp.float32
            )
            last = jnp.where(distance + yl_at * coarse >= 0, scores[:, known:], NEG_FILL)
            if known:
                scores = jnp.concatenate([scores[:, :known], last], axis=1)
            else:
                scores = last
            top = jnp.maximum(jnp.max(scores, axis=1, keepdims=True), NEG_CLAMP) * EXP2_SCALE
            shift = top.astype(jnp.bfloat16).astype(jnp.float32)
            weights = jnp.exp2(scores * EXP2_SCALE - shift)
            weighted = jnp.dot(
                weights.astype(jnp.bfloat16), values, preferred_element_type=jnp.float32
            )
            rounded = weighted.astype(jnp.bfloat16).astype(jnp.float32)
            weighted = jnp.where(lane == TOTAL_LOW, weighted - rounded, weighted)
            weighted = jnp.where(lane == SHIFT, shift, weighted)
            out_ref[start : start + block, :] = weighted.astype(out_ref.dtype)


def attend(queries, keys_values, x_size, rows):
    def body(q_ref, kv_ref, out_ref):
        attend_kernel(x_size, rows, q_ref, kv_ref, out_ref)

    return pl.pallas_call(
        body,
        out_shape=jax.ShapeDtypeStruct(queries.shape, queries.dtype),
        compiler_params=pltpu.CompilerParams(vmem_limit_bytes=VMEM_LIMIT),
    )(queries, keys_values)


def combine(parts_ref, attention_ref, heads, groups, rows):
    for head in range(heads):
        parts = [
            parts_ref[
                (head * groups + group) * rows : (head * groups + group + 1) * rows, :
            ].astype(jnp.float32)
            for group in range(groups)
        ]
        shifts = [part[:, SHIFT : SHIFT + 1] for part in parts]
        top = shifts[0]
        for shift in shifts[1:]:
            top = jnp.maximum(top, shift)
        mixed = jnp.zeros_like(parts[0])
        for shift, part in zip(shifts, parts):
            mixed = mixed + jnp.exp2(shift - top) * part
        row_total = mixed[:, TOTAL : TOTAL + 1] + mixed[:, TOTAL_LOW : TOTAL_LOW + 1]
        attention_ref[:, head * HEAD_DIM : (head + 1) * HEAD_DIM] = (
            mixed[:, :HEAD_DIM] / row_total
        ).astype(attention_ref.dtype)


def share_of(attention_ref, weight_ref, step, tp_size):
    width = weight_ref.shape[1] // tp_size
    member = lax.rem(lax.axis_index("tp") + step, tp_size)
    columns = pl.ds(pl.multiple_of(member * width, LANES), width)
    return jnp.dot(
        attention_ref[...], weight_ref[:, columns], preferred_element_type=jnp.float32
    )


def project_far(parts, out_weight, heads, groups, rows, step, tp_size):
    features, columns = out_weight.shape

    def body(parts_ref, weight_ref, attention_ref, far_ref):
        combine(parts_ref, attention_ref, heads, groups, rows)
        far_ref[...] = share_of(attention_ref, weight_ref, step, tp_size).astype(far_ref.dtype)

    return pl.pallas_call(
        body,
        out_shape=(
            jax.ShapeDtypeStruct((rows, features), jnp.bfloat16),
            jax.ShapeDtypeStruct((rows, columns // tp_size), jnp.bfloat16),
        ),
        cost_estimate=pl.CostEstimate(
            flops=2 * rows * features * columns // tp_size,
            bytes_accessed=2 * features * columns,
            transcendentals=0,
        ),
        compiler_params=pltpu.CompilerParams(vmem_limit_bytes=VMEM_LIMIT),
    )(parts, out_weight)


def project_near(attention, out_weight, steps, tp_size):
    rows, features = attention.shape
    columns = out_weight.shape[1]

    def body(attention_ref, weight_ref, *out_refs):
        for step, out_ref in zip(steps, out_refs):
            out_ref[...] = share_of(attention_ref, weight_ref, step, tp_size).astype(
                out_ref.dtype
            )

    return pl.pallas_call(
        body,
        out_shape=[
            jax.ShapeDtypeStruct(
                (rows, columns // tp_size), jnp.bfloat16 if step else jnp.float32
            )
            for step in steps
        ],
        cost_estimate=pl.CostEstimate(
            flops=2 * rows * features * len(steps) * (columns // tp_size),
            bytes_accessed=2 * features * columns,
            transcendentals=0,
        ),
        compiler_params=pltpu.CompilerParams(vmem_limit_bytes=VMEM_LIMIT),
    )(attention, out_weight)


def to_member(share, step, tp_size):
    return lax.ppermute(share, "tp", [(i, (i + step) % tp_size) for i in range(tp_size)])


def shards(queries, keys, values, out_weight):
    rows, features = queries.shape
    heads = features // HEAD_DIM
    x_size = lax.axis_size("x")
    query_copies = lax.axis_size("yl") * lax.axis_size("zl") * lax.axis_size("core")
    key_copies = lax.axis_size("zh")
    tp_size = lax.axis_size("tp")

    sent_q, sent_kv = pack(queries, keys, values, heads, query_copies, key_copies)
    got_q = lax.all_to_all(
        sent_q.reshape(heads * query_copies, rows, LANES), QUERY_AXES, 0, 0, tiled=True
    )
    got_kv = lax.all_to_all(
        sent_kv.reshape(heads * key_copies, rows, 2 * LANES), KEY_AXES, 0, 0, tiled=True
    )
    partial = attend(
        got_q.reshape(-1, LANES), got_kv.reshape(-1, 2 * LANES), x_size, rows
    )
    returned = lax.all_to_all(
        partial.reshape(heads * query_copies, rows, LANES), QUERY_AXES, 0, 0, tiled=True
    )
    far = tp_size // 2
    near = [step for step in range(1, tp_size) if step != far]
    attention, far_share = project_far(
        returned.reshape(-1, LANES), out_weight, heads, query_copies, rows, far, tp_size
    )
    arrived = [to_member(far_share, far, tp_size)]
    *near_shares, own_share = project_near(attention, out_weight, near + [0], tp_size)
    arrived += [to_member(share, step, tp_size) for share, step in zip(near_shares, near)]
    total = own_share
    for share in arrived:
        total = total + share.astype(jnp.float32)
    return total.astype(jnp.bfloat16)


def solution(mesh):
    split = Mesh(mesh.devices.reshape(4, 2, 4, 2, 2, 4), AXES)
    placed = (P(CTX, "tp"), P(CTX, "tp"), P(CTX, "tp"), P("tp", None))
    return jax.shard_map(
        shards, mesh=split, in_specs=placed, out_specs=P(CTX, "tp"), check_vma=False
    )
```

```python
import math

import jax
import jax.numpy as jnp
from jax import lax
from jax.experimental import pallas as pl
from jax.experimental.pallas import tpu as pltpu
from jax.sharding import Mesh, PartitionSpec as P

HEAD_DIM = 112
LANES = 128
TOTAL, TOTAL_LOW, SHIFT = HEAD_DIM, HEAD_DIM + 1, HEAD_DIM + 2
NEG_FILL = -1e30
AXES = ("x", "yl", "zh", "zl", "core", "tp")
CTX = AXES[:5]
HEAD_AXES = ("zl", "core")
QUERY_AXES = ("x", "yl")
RETURN_AXES = ("x", "yl", "zl", "core")
VMEM_LIMIT = 48 * 1024 * 1024
EXP2_SCALE = math.log2(math.e) / HEAD_DIM**0.5


def pack(queries, keys, values, heads):
    rows = queries.shape[0]
    kind = queries.dtype

    def body(held, out_ref):
        for head in range(heads):
            columns = slice(head * HEAD_DIM, (head + 1) * HEAD_DIM)
            key, value, query = (
                held[part * rows : (part + 1) * rows, columns] for part in range(3)
            )
            gap = jnp.zeros((rows, LANES - HEAD_DIM), kind)
            out_ref[head] = jnp.concatenate(
                [key, gap, value, jnp.ones_like(gap), query, gap], axis=1
            )

    return pl.pallas_call(
        body,
        out_shape=jax.ShapeDtypeStruct((heads, rows, 3 * LANES), kind),
        compiler_params=pltpu.CompilerParams(vmem_limit_bytes=VMEM_LIMIT),
    )(jnp.concatenate([keys, values, queries], axis=0))


def spread(one_head, copies):
    rows = one_head.shape[0]
    kind = one_head.dtype

    def body(one_ref, kv_out, q_out):
        kv_out[...] = one_ref[:, : 2 * LANES]
        query = one_ref[:, 2 * LANES :]
        for copy in range(copies):
            q_out[copy] = query

    return pl.pallas_call(
        body,
        out_shape=(
            jax.ShapeDtypeStruct((rows, 2 * LANES), kind),
            jax.ShapeDtypeStruct((copies, rows, LANES), kind),
        ),
        compiler_params=pltpu.CompilerParams(vmem_limit_bytes=VMEM_LIMIT),
    )(one_head)


def attend_kernel(coarse_size, steps, block, q_ref, kv_refs, out_ref):
    zh_size = lax.axis_size("zh")
    zh = lax.axis_index("zh")
    own_coarse = lax.axis_index("x") * lax.axis_size("yl") + lax.axis_index("yl")
    lane = lax.broadcasted_iota(jnp.int32, (block, LANES), 1)

    def tile(at, masked):
        start = pl.multiple_of(at * block, block)
        queries = q_ref[pl.ds(start, block), :]
        scores = []
        for step, kv_ref in zip(steps, kv_refs):
            part = lax.dot_general(
                queries,
                kv_ref[:, :LANES],
                (((1,), (1,)), ((), ())),
                preferred_element_type=jnp.float32,
            )
            if masked:
                source = lax.rem(zh + zh_size - step, zh_size)
                query_at = lax.broadcasted_iota(jnp.int32, (block, block), 0)
                key_at = lax.broadcasted_iota(jnp.int32, (block, block), 1)
                part = jnp.where(
                    query_at - key_at + (zh - source) * block >= 0, part, NEG_FILL
                )
            scores.append(part)
        scores = jnp.concatenate(scores, axis=1)
        top = jnp.max(scores, axis=1, keepdims=True) * EXP2_SCALE
        shift = top.astype(jnp.bfloat16).astype(jnp.float32)
        weights = jnp.exp2(scores * EXP2_SCALE - shift).astype(jnp.bfloat16)
        weighted = jnp.zeros((block, LANES), jnp.float32)
        for part, kv_ref in enumerate(kv_refs):
            weighted = weighted + jnp.dot(
                weights[:, part * block : (part + 1) * block],
                kv_ref[:, LANES:],
                preferred_element_type=jnp.float32,
            )
        rounded = weighted.astype(jnp.bfloat16).astype(jnp.float32)
        weighted = jnp.where(lane == TOTAL_LOW, weighted - rounded, weighted)
        weighted = jnp.where(lane == SHIFT, shift, weighted)
        out_ref[pl.ds(start, block), :] = weighted.astype(out_ref.dtype)

    for at in range(coarse_size):

        @pl.when(at > own_coarse)
        def _(at=at):
            tile(at, False)

        @pl.when(at == own_coarse)
        def _(at=at):
            tile(at, True)

        @pl.when(at < own_coarse)
        def _(at=at):
            out_ref[at * block : (at + 1) * block, :] = jnp.where(
                lane == SHIFT, NEG_FILL, 0.0
            ).astype(out_ref.dtype)


def attend(queries, keys_values, steps, coarse_size):
    block = queries.shape[0] // coarse_size

    def body(q_ref, *refs):
        attend_kernel(coarse_size, steps, block, q_ref, refs[:-1], refs[-1])

    return pl.pallas_call(
        body,
        out_shape=jax.ShapeDtypeStruct(queries.shape, queries.dtype),
        compiler_params=pltpu.CompilerParams(vmem_limit_bytes=VMEM_LIMIT),
    )(queries, *keys_values)


def combine(parts_ref, attention_ref, heads, groups, rows):
    for head in range(heads):
        parts = [
            parts_ref[
                (group * heads + head) * rows : (group * heads + head + 1) * rows, :
            ].astype(jnp.float32)
            for group in range(groups)
        ]
        shifts = [part[:, SHIFT : SHIFT + 1] for part in parts]
        top = shifts[0]
        for shift in shifts[1:]:
            top = jnp.maximum(top, shift)
        mixed = jnp.zeros_like(parts[0])
        for shift, part in zip(shifts, parts):
            mixed = mixed + jnp.exp2(shift - top) * part
        row_total = mixed[:, TOTAL : TOTAL + 1] + mixed[:, TOTAL_LOW : TOTAL_LOW + 1]
        attention_ref[:, head * HEAD_DIM : (head + 1) * HEAD_DIM] = (
            mixed[:, :HEAD_DIM] / row_total
        ).astype(attention_ref.dtype)


def share_of(attention_ref, weight_ref, step, tp_size):
    width = weight_ref.shape[1] // tp_size
    member = lax.rem(lax.axis_index("tp") + step, tp_size)
    columns = pl.ds(pl.multiple_of(member * width, LANES), width)
    return jnp.dot(
        attention_ref[...], weight_ref[:, columns], preferred_element_type=jnp.float32
    )


def project_far(parts, out_weight, heads, groups, rows, step, tp_size):
    features, columns = out_weight.shape

    def body(parts_ref, weight_ref, attention_ref, far_ref):
        combine(parts_ref, attention_ref, heads, groups, rows)
        far_ref[...] = share_of(attention_ref, weight_ref, step, tp_size).astype(far_ref.dtype)

    return pl.pallas_call(
        body,
        out_shape=(
            jax.ShapeDtypeStruct((rows, features), jnp.bfloat16),
            jax.ShapeDtypeStruct((rows, columns // tp_size), jnp.bfloat16),
        ),
        cost_estimate=pl.CostEstimate(
            flops=2 * rows * features * columns // tp_size,
            bytes_accessed=2 * features * columns,
            transcendentals=0,
        ),
        compiler_params=pltpu.CompilerParams(vmem_limit_bytes=VMEM_LIMIT),
    )(parts, out_weight)


def project_near(attention, out_weight, steps, tp_size):
    rows, features = attention.shape
    columns = out_weight.shape[1]

    def body(attention_ref, weight_ref, *out_refs):
        for step, out_ref in zip(steps, out_refs):
            out_ref[...] = share_of(attention_ref, weight_ref, step, tp_size).astype(
                out_ref.dtype
            )

    return pl.pallas_call(
        body,
        out_shape=[
            jax.ShapeDtypeStruct(
                (rows, columns // tp_size), jnp.bfloat16 if step else jnp.float32
            )
            for step in steps
        ],
        cost_estimate=pl.CostEstimate(
            flops=2 * rows * features * len(steps) * (columns // tp_size),
            bytes_accessed=2 * features * columns,
            transcendentals=0,
        ),
        compiler_params=pltpu.CompilerParams(vmem_limit_bytes=VMEM_LIMIT),
    )(attention, out_weight)


def to_member(share, step, tp_size):
    return lax.ppermute(share, "tp", [(i, (i + step) % tp_size) for i in range(tp_size)])


def shards(queries, keys, values, out_weight):
    rows, features = queries.shape
    heads = features // HEAD_DIM
    coarse_size = lax.axis_size("x") * lax.axis_size("yl")
    zh_size = lax.axis_size("zh")
    tp_size = lax.axis_size("tp")

    one_head = lax.all_to_all(
        pack(queries, keys, values, heads), HEAD_AXES, 0, 0, tiled=True
    ).reshape(heads * rows, 3 * LANES)
    own_kv, sent_q = spread(one_head, coarse_size)
    steps = [0, zh_size // 2] + [step for step in range(1, zh_size) if step != zh_size // 2]
    got_kv = [own_kv] + [
        lax.ppermute(own_kv, "zh", [(i, (i + step) % zh_size) for i in range(zh_size)])
        for step in steps[1:]
    ]
    got_q = lax.all_to_all(sent_q, QUERY_AXES, 0, 0, tiled=True)
    partial = attend(got_q.reshape(-1, LANES), got_kv, steps, coarse_size)
    returned = lax.all_to_all(
        partial.reshape(coarse_size * heads, rows, LANES), RETURN_AXES, 0, 0, tiled=True
    )
    far = tp_size // 2
    near = [step for step in range(1, tp_size) if step != far]
    attention, far_share = project_far(
        returned.reshape(-1, LANES), out_weight, heads, coarse_size, rows, far, tp_size
    )
    arrived = [to_member(far_share, far, tp_size)]
    *near_shares, own_share = project_near(attention, out_weight, near + [0], tp_size)
    arrived += [to_member(share, step, tp_size) for share, step in zip(near_shares, near)]
    total = own_share
    for share in arrived:
        total = total + share.astype(jnp.float32)
    return total.astype(jnp.bfloat16)


def solution(mesh):
    split = Mesh(mesh.devices.reshape(4, 2, 4, 2, 2, 4), AXES)
    placed = (P(CTX, "tp"), P(CTX, "tp"), P(CTX, "tp"), P("tp", None))
    return jax.shard_map(
        shards, mesh=split, in_specs=placed, out_specs=P(CTX, "tp"), check_vma=False
    )
```

```python
import math

import jax
import jax.numpy as jnp
from jax import lax
from jax.experimental import pallas as pl
from jax.experimental.pallas import tpu as pltpu
from jax.sharding import Mesh, PartitionSpec as P

HEAD_DIM = 112
LANES = 128
TOTAL, TOTAL_LOW, SHIFT = HEAD_DIM, HEAD_DIM + 1, HEAD_DIM + 2
NEG_FILL = -1e30
AXES = ("x", "yl", "zh", "zl", "core", "tp")
CTX = AXES[:5]
HEAD_AXES = ("zl", "core")
QUERY_AXES = ("x", "yl")
RETURN_AXES = ("x", "yl", "zl", "core")
VMEM_LIMIT = 48 * 1024 * 1024
VMEM_MOST = 58 * 1024 * 1024
VMEM_WHOLE = 63 * 1024 * 1024
EXP2_SCALE = math.log2(math.e) / HEAD_DIM**0.5


def pack(queries, keys, values, heads):
    rows = queries.shape[0]
    kind = queries.dtype

    def body(held, out_ref):
        for head in range(heads):
            columns = slice(head * HEAD_DIM, (head + 1) * HEAD_DIM)
            key, value, query = (
                held[part * rows : (part + 1) * rows, columns] for part in range(3)
            )
            gap = jnp.zeros((rows, LANES - HEAD_DIM), kind)
            out_ref[head] = jnp.concatenate(
                [key, gap, value, jnp.ones_like(gap), query, gap], axis=1
            )

    return pl.pallas_call(
        body,
        out_shape=jax.ShapeDtypeStruct((heads, rows, 3 * LANES), kind),
        compiler_params=pltpu.CompilerParams(vmem_limit_bytes=VMEM_LIMIT),
    )(jnp.concatenate([keys, values, queries], axis=0))


def spread(one_head, copies):
    rows = one_head.shape[0]
    kind = one_head.dtype

    def body(one_ref, kv_out, q_out):
        kv_out[...] = one_ref[:, : 2 * LANES]
        query = one_ref[:, 2 * LANES :]
        for copy in range(copies):
            q_out[copy] = query

    return pl.pallas_call(
        body,
        out_shape=(
            jax.ShapeDtypeStruct((rows, 2 * LANES), kind),
            jax.ShapeDtypeStruct((copies, rows, LANES), kind),
        ),
        compiler_params=pltpu.CompilerParams(vmem_limit_bytes=VMEM_WHOLE),
    )(one_head)


def attend_kernel(coarse_size, steps, block, q_ref, kv_refs, out_ref):
    zh_size = lax.axis_size("zh")
    zh = lax.axis_index("zh")
    own_coarse = lax.axis_index("x") * lax.axis_size("yl") + lax.axis_index("yl")
    lane = lax.broadcasted_iota(jnp.int32, (block, LANES), 1)

    def tile(at, masked):
        start = pl.multiple_of(at * block, block)
        queries = q_ref[pl.ds(start, block), :]
        scores = []
        for step, kv_ref in zip(steps, kv_refs):
            part = lax.dot_general(
                queries,
                kv_ref[:, :LANES],
                (((1,), (1,)), ((), ())),
                preferred_element_type=jnp.float32,
            )
            if masked:
                source = lax.rem(zh + zh_size - step, zh_size)
                query_at = lax.broadcasted_iota(jnp.int32, (block, block), 0)
                key_at = lax.broadcasted_iota(jnp.int32, (block, block), 1)
                part = jnp.where(
                    query_at - key_at + (zh - source) * block >= 0, part, NEG_FILL
                )
            scores.append(part)
        scores = jnp.concatenate(scores, axis=1)
        top = jnp.max(scores, axis=1, keepdims=True) * EXP2_SCALE
        shift = top.astype(jnp.bfloat16).astype(jnp.float32)
        weights = jnp.exp2(scores * EXP2_SCALE - shift).astype(jnp.bfloat16)
        weighted = jnp.zeros((block, LANES), jnp.float32)
        for part, kv_ref in enumerate(kv_refs):
            weighted = weighted + jnp.dot(
                weights[:, part * block : (part + 1) * block],
                kv_ref[:, LANES:],
                preferred_element_type=jnp.float32,
            )
        rounded = weighted.astype(jnp.bfloat16).astype(jnp.float32)
        weighted = jnp.where(lane == TOTAL_LOW, weighted - rounded, weighted)
        weighted = jnp.where(lane == SHIFT, shift, weighted)
        out_ref[pl.ds(start, block), :] = weighted.astype(out_ref.dtype)

    def empty(at, _):
        start = pl.multiple_of(at * block, block)
        out_ref[pl.ds(start, block), :] = jnp.where(lane == SHIFT, NEG_FILL, 0.0).astype(
            out_ref.dtype
        )
        return 0

    def pair(count, first):
        tile(first + 2 * count, False)
        tile(first + 2 * count + 1, False)
        return first

    lax.fori_loop(0, own_coarse, empty, 0)
    later = coarse_size - 1 - own_coarse
    odd = lax.rem(later, 2)

    @pl.when(odd == 1)
    def _():
        tile(own_coarse, True)
        tile(own_coarse + 1, False)

    @pl.when(odd == 0)
    def _():
        tile(own_coarse, True)

    lax.fori_loop(0, later // 2, pair, own_coarse + 1 + odd)


def attend(queries, keys_values, steps, coarse_size):
    block = queries.shape[0] // coarse_size

    def body(q_ref, *refs):
        attend_kernel(coarse_size, steps, block, q_ref, refs[:-1], refs[-1])

    return pl.pallas_call(
        body,
        out_shape=jax.ShapeDtypeStruct(queries.shape, queries.dtype),
        compiler_params=pltpu.CompilerParams(vmem_limit_bytes=VMEM_MOST),
    )(queries, *keys_values)


def combine(parts_ref, attention_ref, heads, groups, rows):
    for head in range(heads):
        parts = [
            parts_ref[
                (group * heads + head) * rows : (group * heads + head + 1) * rows, :
            ].astype(jnp.float32)
            for group in range(groups)
        ]
        shifts = [part[:, SHIFT : SHIFT + 1] for part in parts]
        top = shifts[0]
        for shift in shifts[1:]:
            top = jnp.maximum(top, shift)
        mixed = jnp.zeros_like(parts[0])
        for shift, part in zip(shifts, parts):
            mixed = mixed + jnp.exp2(shift - top) * part
        row_total = mixed[:, TOTAL : TOTAL + 1] + mixed[:, TOTAL_LOW : TOTAL_LOW + 1]
        attention_ref[:, head * HEAD_DIM : (head + 1) * HEAD_DIM] = (
            mixed[:, :HEAD_DIM] / row_total
        ).astype(attention_ref.dtype)


def share_of(attention_ref, weight_ref, step, tp_size):
    width = weight_ref.shape[1] // tp_size
    member = lax.rem(lax.axis_index("tp") + step, tp_size)
    columns = pl.ds(pl.multiple_of(member * width, LANES), width)
    return jnp.dot(
        attention_ref[...], weight_ref[:, columns], preferred_element_type=jnp.float32
    )


def project_far(parts, out_weight, heads, groups, rows, step, tp_size):
    features, columns = out_weight.shape

    def body(parts_ref, weight_ref, attention_ref, far_ref):
        combine(parts_ref, attention_ref, heads, groups, rows)
        far_ref[...] = share_of(attention_ref, weight_ref, step, tp_size).astype(far_ref.dtype)

    return pl.pallas_call(
        body,
        out_shape=(
            jax.ShapeDtypeStruct((rows, features), jnp.bfloat16),
            jax.ShapeDtypeStruct((rows, columns // tp_size), jnp.bfloat16),
        ),
        cost_estimate=pl.CostEstimate(
            flops=2 * rows * features * columns // tp_size,
            bytes_accessed=2 * features * columns,
            transcendentals=0,
        ),
        compiler_params=pltpu.CompilerParams(vmem_limit_bytes=VMEM_LIMIT),
    )(parts, out_weight)


def project_near(attention, out_weight, steps, tp_size):
    rows, features = attention.shape
    columns = out_weight.shape[1]

    def body(attention_ref, weight_ref, *out_refs):
        for step, out_ref in zip(steps, out_refs):
            out_ref[...] = share_of(attention_ref, weight_ref, step, tp_size).astype(
                out_ref.dtype
            )

    return pl.pallas_call(
        body,
        out_shape=[
            jax.ShapeDtypeStruct(
                (rows, columns // tp_size), jnp.bfloat16 if step else jnp.float32
            )
            for step in steps
        ],
        cost_estimate=pl.CostEstimate(
            flops=2 * rows * features * len(steps) * (columns // tp_size),
            bytes_accessed=2 * features * columns,
            transcendentals=0,
        ),
        compiler_params=pltpu.CompilerParams(vmem_limit_bytes=VMEM_LIMIT),
    )(attention, out_weight)


def to_member(share, step, tp_size):
    return lax.ppermute(share, "tp", [(i, (i + step) % tp_size) for i in range(tp_size)])


def shards(queries, keys, values, out_weight):
    rows, features = queries.shape
    heads = features // HEAD_DIM
    coarse_size = lax.axis_size("x") * lax.axis_size("yl")
    zh_size = lax.axis_size("zh")
    tp_size = lax.axis_size("tp")

    one_head = lax.all_to_all(
        pack(queries, keys, values, heads), HEAD_AXES, 0, 0, tiled=True
    ).reshape(heads * rows, 3 * LANES)
    own_kv, sent_q = spread(one_head, coarse_size)
    steps = [0, zh_size // 2] + [step for step in range(1, zh_size) if step != zh_size // 2]
    got_kv = [own_kv] + [
        lax.ppermute(own_kv, "zh", [(i, (i + step) % zh_size) for i in range(zh_size)])
        for step in steps[1:]
    ]
    got_q = lax.all_to_all(sent_q, QUERY_AXES, 0, 0, tiled=True)
    partial = attend(got_q.reshape(-1, LANES), got_kv, steps, coarse_size)
    returned = lax.all_to_all(
        partial.reshape(coarse_size * heads, rows, LANES), RETURN_AXES, 0, 0, tiled=True
    )
    far = tp_size // 2
    near = [step for step in range(1, tp_size) if step != far]
    attention, far_share = project_far(
        returned.reshape(-1, LANES), out_weight, heads, coarse_size, rows, far, tp_size
    )
    arrived = [to_member(far_share, far, tp_size)]
    *near_shares, own_share = project_near(attention, out_weight, near + [0], tp_size)
    arrived += [to_member(share, step, tp_size) for share, step in zip(near_shares, near)]
    total = own_share
    for share in arrived:
        total = total + share.astype(jnp.float32)
    return total.astype(jnp.bfloat16)


def solution(mesh):
    split = Mesh(mesh.devices.reshape(4, 2, 4, 2, 2, 4), AXES)
    placed = (P(CTX, "tp"), P(CTX, "tp"), P(CTX, "tp"), P("tp", None))
    return jax.shard_map(
        shards, mesh=split, in_specs=placed, out_specs=P(CTX, "tp"), check_vma=False
    )
```

```python
import math

import jax
import jax.numpy as jnp
from jax import lax
from jax.experimental import pallas as pl
from jax.experimental.pallas import tpu as pltpu
from jax.sharding import Mesh, PartitionSpec as P

HEAD_DIM = 112
LANES = 128
TOTAL, TOTAL_LOW, SHIFT = HEAD_DIM, HEAD_DIM + 1, HEAD_DIM + 2
NEG_FILL = -1e30
NEG_CLAMP = -1e29
AXES = ("x", "yl", "zh", "zl", "core", "tp")
CTX = AXES[:5]
QUERY_AXES = ("x", "yl", "zl", "core")
KEY_AXES = ("x", "zh")
VMEM_LIMIT = 48 * 1024 * 1024
EXP2_SCALE = math.log2(math.e) / HEAD_DIM**0.5


def pack_kernel(rows, held, q_out, kv_out):
    for head in range(q_out.shape[0]):
        columns = slice(head * HEAD_DIM, (head + 1) * HEAD_DIM)
        key, value, query = (
            held[part * rows : (part + 1) * rows, columns] for part in range(3)
        )
        gap = jnp.zeros((rows, LANES - HEAD_DIM), key.dtype)
        pair = jnp.concatenate([key, gap, value, jnp.ones_like(gap)], axis=1)
        query = jnp.concatenate([query, gap], axis=1)
        for copy in range(kv_out.shape[1]):
            kv_out[head, copy] = pair
        for copy in range(q_out.shape[1]):
            q_out[head, copy] = query


def pack(queries, keys, values, heads, query_copies, key_copies):
    rows = queries.shape[0]
    kind = queries.dtype

    def body(held, q_out, kv_out):
        pack_kernel(rows, held, q_out, kv_out)

    return pl.pallas_call(
        body,
        out_shape=(
            jax.ShapeDtypeStruct((heads, query_copies, rows, LANES), kind),
            jax.ShapeDtypeStruct((heads, key_copies, rows, 2 * LANES), kind),
        ),
        compiler_params=pltpu.CompilerParams(vmem_limit_bytes=VMEM_LIMIT),
    )(jnp.concatenate([keys, values, queries], axis=0))


def attend_kernel(x_size, rows, q_ref, kv_ref, out_ref):
    yl, zh, zl, core = (lax.axis_index(name) for name in ("yl", "zh", "zl", "core"))
    block = 4 * rows
    coarse = 16 * rows
    delta = zh * block - yl * coarse - zl * 2 * rows - core * rows
    query_at = lax.broadcasted_iota(jnp.int32, (block, block), 0)
    key_at = lax.broadcasted_iota(jnp.int32, (block, block), 1)
    key_at = (key_at // rows) * block + key_at % rows
    distance = query_at - key_at + delta
    lane = lax.broadcasted_iota(jnp.int32, (block, LANES), 1)
    for x_at in range(x_size):
        known = x_at * block
        total = known + block
        keys = kv_ref[:total, :LANES]
        values = kv_ref[:total, LANES:]
        for yl_at in range(2):
            start = (x_at * 2 + yl_at) * block
            queries = q_ref[start : start + block, :]
            scores = lax.dot_general(
                queries, keys, (((1,), (1,)), ((), ())), preferred_element_type=jnp.float32
            )
            last = jnp.where(distance + yl_at * coarse >= 0, scores[:, known:], NEG_FILL)
            if known:
                scores = jnp.concatenate([scores[:, :known], last], axis=1)
            else:
                scores = last
            top = jnp.maximum(jnp.max(scores, axis=1, keepdims=True), NEG_CLAMP) * EXP2_SCALE
            shift = top.astype(jnp.bfloat16).astype(jnp.float32)
            weights = jnp.exp2(scores * EXP2_SCALE - shift)
            weighted = jnp.dot(
                weights.astype(jnp.bfloat16), values, preferred_element_type=jnp.float32
            )
            rounded = weighted.astype(jnp.bfloat16).astype(jnp.float32)
            weighted = jnp.where(lane == TOTAL_LOW, weighted - rounded, weighted)
            weighted = jnp.where(lane == SHIFT, shift, weighted)
            out_ref[start : start + block, :] = weighted.astype(out_ref.dtype)


def attend(queries, keys_values, x_size, rows):
    def body(q_ref, kv_ref, out_ref):
        attend_kernel(x_size, rows, q_ref, kv_ref, out_ref)

    return pl.pallas_call(
        body,
        out_shape=jax.ShapeDtypeStruct(queries.shape, queries.dtype),
        compiler_params=pltpu.CompilerParams(vmem_limit_bytes=VMEM_LIMIT),
    )(queries, keys_values)


def combine(parts_ref, attention_ref, heads, groups, rows):
    for head in range(heads):
        parts = [
            parts_ref[
                (head * groups + group) * rows : (head * groups + group + 1) * rows, :
            ].astype(jnp.float32)
            for group in range(groups)
        ]
        shifts = [part[:, SHIFT : SHIFT + 1] for part in parts]
        top = shifts[0]
        for shift in shifts[1:]:
            top = jnp.maximum(top, shift)
        mixed = jnp.zeros_like(parts[0])
        for shift, part in zip(shifts, parts):
            mixed = mixed + jnp.exp2(shift - top) * part
        row_total = mixed[:, TOTAL : TOTAL + 1] + mixed[:, TOTAL_LOW : TOTAL_LOW + 1]
        attention_ref[:, head * HEAD_DIM : (head + 1) * HEAD_DIM] = (
            mixed[:, :HEAD_DIM] / row_total
        ).astype(attention_ref.dtype)


def share_of(attention_ref, weight_ref, step, tp_size):
    width = weight_ref.shape[1] // tp_size
    member = lax.rem(lax.axis_index("tp") + step, tp_size)
    columns = pl.ds(pl.multiple_of(member * width, LANES), width)
    return jnp.dot(
        attention_ref[...], weight_ref[:, columns], preferred_element_type=jnp.float32
    )


def project_far(parts, out_weight, heads, groups, rows, step, tp_size):
    features, columns = out_weight.shape
    width = columns // tp_size
    half = rows // 2

    def body(parts_ref, weight_ref, attention_ref, upper_ref, lower_ref):
        combine(parts_ref, attention_ref, heads, groups, rows)
        share = share_of(attention_ref, weight_ref, step, tp_size).astype(upper_ref.dtype)
        upper_ref[...] = share[:half]
        lower_ref[...] = share[half:]

    return pl.pallas_call(
        body,
        out_shape=(
            jax.ShapeDtypeStruct((rows, features), jnp.bfloat16),
            jax.ShapeDtypeStruct((half, width), jnp.bfloat16),
            jax.ShapeDtypeStruct((half, width), jnp.bfloat16),
        ),
        cost_estimate=pl.CostEstimate(
            flops=2 * rows * features * width,
            bytes_accessed=2 * features * columns,
            transcendentals=0,
        ),
        compiler_params=pltpu.CompilerParams(vmem_limit_bytes=VMEM_LIMIT),
    )(parts, out_weight)


def project_near(attention, out_weight, steps, tp_size):
    rows, features = attention.shape
    columns = out_weight.shape[1]

    def body(attention_ref, weight_ref, *out_refs):
        for step, out_ref in zip(steps, out_refs):
            out_ref[...] = share_of(attention_ref, weight_ref, step, tp_size)

    return pl.pallas_call(
        body,
        out_shape=[
            jax.ShapeDtypeStruct((rows, columns // tp_size), jnp.float32) for _ in steps
        ],
        cost_estimate=pl.CostEstimate(
            flops=2 * rows * features * len(steps) * (columns // tp_size),
            bytes_accessed=2 * features * columns,
            transcendentals=0,
        ),
        compiler_params=pltpu.CompilerParams(vmem_limit_bytes=VMEM_LIMIT),
    )(attention, out_weight)


def add_passing(up, down, upper, lower):
    half = upper.shape[0]

    def body(up_ref, down_ref, upper_ref, lower_ref, up_out, down_out):
        up_out[:half] = (up_ref[:half] + upper_ref[...].astype(jnp.float32)).astype(up_out.dtype)
        up_out[half:] = up_ref[half:].astype(up_out.dtype)
        down_out[:half] = down_ref[:half].astype(down_out.dtype)
        down_out[half:] = (down_ref[half:] + lower_ref[...].astype(jnp.float32)).astype(
            down_out.dtype
        )

    return pl.pallas_call(
        body,
        out_shape=[jax.ShapeDtypeStruct(up.shape, jnp.bfloat16)] * 2,
        compiler_params=pltpu.CompilerParams(vmem_limit_bytes=VMEM_LIMIT),
    )(up, down, upper, lower)


def to_member(share, step, tp_size):
    return lax.ppermute(share, "tp", [(i, (i + step) % tp_size) for i in range(tp_size)])


def shards(queries, keys, values, out_weight):
    rows, features = queries.shape
    heads = features // HEAD_DIM
    x_size = lax.axis_size("x")
    query_copies = lax.axis_size("yl") * lax.axis_size("zl") * lax.axis_size("core")
    key_copies = lax.axis_size("zh")
    tp_size = lax.axis_size("tp")

    sent_q, sent_kv = pack(queries, keys, values, heads, query_copies, key_copies)
    got_q = lax.all_to_all(
        sent_q.reshape(heads * query_copies, rows, LANES), QUERY_AXES, 0, 0, tiled=True
    )
    got_kv = lax.all_to_all(
        sent_kv.reshape(heads * key_copies, rows, 2 * LANES), KEY_AXES, 0, 0, tiled=True
    )
    partial = attend(
        got_q.reshape(-1, LANES), got_kv.reshape(-1, 2 * LANES), x_size, rows
    )
    returned = lax.all_to_all(
        partial.reshape(heads * query_copies, rows, LANES), QUERY_AXES, 0, 0, tiled=True
    )
    attention, upper, lower = project_far(
        returned.reshape(-1, LANES), out_weight, heads, query_copies, rows, 2, tp_size
    )
    upper = to_member(upper, 1, tp_size)
    lower = to_member(lower, 3, tp_size)
    up, down, own_share = project_near(attention, out_weight, (1, 3, 0), tp_size)
    up, down = add_passing(up, down, upper, lower)
    up = to_member(up, 1, tp_size)
    down = to_member(down, 3, tp_size)
    total = own_share + up.astype(jnp.float32) + down.astype(jnp.float32)
    return total.astype(jnp.bfloat16)


def solution(mesh):
    split = Mesh(mesh.devices.reshape(4, 2, 4, 2, 2, 4), AXES)
    placed = (P(CTX, "tp"), P(CTX, "tp"), P(CTX, "tp"), P("tp", None))
    return jax.shard_map(
        shards, mesh=split, in_specs=placed, out_specs=P(CTX, "tp"), check_vma=False
    )
```

```python
import math

import jax
import jax.numpy as jnp
from jax import lax
from jax.experimental import pallas as pl
from jax.experimental.pallas import tpu as pltpu
from jax.sharding import Mesh, PartitionSpec as P

HEAD_DIM = 112
LANES = 128
TOTAL, TOTAL_LOW, SHIFT = HEAD_DIM, HEAD_DIM + 1, HEAD_DIM + 2
NEG_FILL = -1e30
NEG_CLAMP = -1e29
AXES = ("xa", "xb", "yl", "zh", "zl", "core", "tp")
CTX = AXES[:6]
HEAD_AXES = ("xa", "zl")
QUERY_AXES = ("xb", "yl", "core")
RETURN_AXES = QUERY_AXES + HEAD_AXES
VMEM_LIMIT = 48 * 1024 * 1024
EXP2_SCALE = math.log2(math.e) / HEAD_DIM**0.5


def pack(queries, keys, values, heads):
    rows = queries.shape[0]
    kind = queries.dtype

    def body(held, out_ref):
        for head in range(heads):
            columns = slice(head * HEAD_DIM, (head + 1) * HEAD_DIM)
            key, value, query = (
                held[part * rows : (part + 1) * rows, columns] for part in range(3)
            )
            gap = jnp.zeros((rows, LANES - HEAD_DIM), kind)
            out_ref[head] = jnp.concatenate(
                [key, gap, value, jnp.ones_like(gap), query, gap], axis=1
            )

    return pl.pallas_call(
        body,
        out_shape=jax.ShapeDtypeStruct((heads, rows, 3 * LANES), kind),
        compiler_params=pltpu.CompilerParams(vmem_limit_bytes=VMEM_LIMIT),
    )(jnp.concatenate([keys, values, queries], axis=0))


def spread(one_head, copies):
    rows = one_head.shape[0]
    kind = one_head.dtype

    def body(one_ref, kv_out, q_out):
        kv_out[...] = one_ref[:, : 2 * LANES]
        query = one_ref[:, 2 * LANES :]
        for copy in range(copies):
            q_out[copy] = query

    return pl.pallas_call(
        body,
        out_shape=(
            jax.ShapeDtypeStruct((rows, 2 * LANES), kind),
            jax.ShapeDtypeStruct((copies, rows, LANES), kind),
        ),
        compiler_params=pltpu.CompilerParams(vmem_limit_bytes=VMEM_LIMIT),
    )(one_head)


def attend_kernel(rows, q_ref, kv_ref, out_ref, key_ref, value_ref):
    xb, yl, zh, core = (lax.axis_index(name) for name in ("xb", "yl", "zh", "core"))
    pair = 2 * rows
    block = 2 * pair
    zh_size = kv_ref.shape[0] // block
    half = zh_size * pair
    coarse = 4 * block
    for xa_at in range(2):
        for zh_at in range(zh_size):
            start = zh_at * block + xa_at * pair
            to_rows = slice(xa_at * half + zh_at * pair, xa_at * half + (zh_at + 1) * pair)
            key_ref[to_rows, :] = kv_ref[start : start + pair, :LANES]
            value_ref[to_rows, :] = kv_ref[start : start + pair, LANES:]
    query_at = lax.broadcasted_iota(jnp.int32, (block, half), 0)
    query_at = query_at % pair + (query_at // rows % 2) * rows + (query_at // pair) * rows
    key_at = lax.broadcasted_iota(jnp.int32, (block, half), 1)
    key_at = (key_at // pair) * block + key_at % pair + (key_at // rows % 2) * rows
    distance = query_at - key_at + zh * block - core * rows
    lane = lax.broadcasted_iota(jnp.int32, (block, LANES), 1)
    for xb_at in range(2):
        for yl_at in range(2):
            ahead = (xb_at - xb) * 2 * coarse + (yl_at - yl) * coarse
            kept = distance + ahead >= 0
            for xa_at in range(2):
                total = (xa_at + 1) * half
                known = total - half
                starts = [
                    ((xb_at * 2 + yl_at) * 2 + core_at) * block + xa_at * pair
                    for core_at in range(2)
                ]
                queries = jnp.concatenate(
                    [q_ref[start : start + pair, :] for start in starts], axis=0
                )
                scores = lax.dot_general(
                    queries,
                    key_ref[:total, :],
                    (((1,), (1,)), ((), ())),
                    preferred_element_type=jnp.float32,
                )
                last = jnp.where(kept, scores[:, known:], NEG_FILL)
                if known:
                    scores = jnp.concatenate([scores[:, :known], last], axis=1)
                else:
                    scores = last
                top = jnp.maximum(jnp.max(scores, axis=1, keepdims=True), NEG_CLAMP)
                shift = (top * EXP2_SCALE).astype(jnp.bfloat16).astype(jnp.float32)
                weights = jnp.exp2(scores * EXP2_SCALE - shift)
                weighted = jnp.dot(
                    weights.astype(jnp.bfloat16),
                    value_ref[:total, :],
                    preferred_element_type=jnp.float32,
                )
                rounded = weighted.astype(jnp.bfloat16).astype(jnp.float32)
                weighted = jnp.where(lane == TOTAL_LOW, weighted - rounded, weighted)
                weighted = jnp.where(lane == SHIFT, shift, weighted).astype(out_ref.dtype)
                for core_at, start in enumerate(starts):
                    out_ref[start : start + pair, :] = weighted[
                        core_at * pair : (core_at + 1) * pair
                    ]


def attend(queries, keys_values, rows):
    def body(*refs):
        attend_kernel(rows, *refs)

    return pl.pallas_call(
        body,
        out_shape=jax.ShapeDtypeStruct(queries.shape, queries.dtype),
        scratch_shapes=[pltpu.VMEM((keys_values.shape[0], LANES), queries.dtype)] * 2,
        compiler_params=pltpu.CompilerParams(vmem_limit_bytes=VMEM_LIMIT),
    )(queries, keys_values)


def combine(parts_ref, attention_ref, heads, groups, rows):
    for head in range(heads):
        parts = [
            parts_ref[
                (group * heads + head) * rows : (group * heads + head + 1) * rows, :
            ].astype(jnp.float32)
            for group in range(groups)
        ]
        shifts = [part[:, SHIFT : SHIFT + 1] for part in parts]
        top = shifts[0]
        for shift in shifts[1:]:
            top = jnp.maximum(top, shift)
        mixed = jnp.zeros_like(parts[0])
        for shift, part in zip(shifts, parts):
            mixed = mixed + jnp.exp2(shift - top) * part
        row_total = mixed[:, TOTAL : TOTAL + 1] + mixed[:, TOTAL_LOW : TOTAL_LOW + 1]
        attention_ref[:, head * HEAD_DIM : (head + 1) * HEAD_DIM] = (
            mixed[:, :HEAD_DIM] / row_total
        ).astype(attention_ref.dtype)


def share_of(attention_ref, weight_ref, step, tp_size):
    width = weight_ref.shape[1] // tp_size
    member = lax.rem(lax.axis_index("tp") + step, tp_size)
    columns = pl.ds(pl.multiple_of(member * width, LANES), width)
    return jnp.dot(
        attention_ref[...], weight_ref[:, columns], preferred_element_type=jnp.float32
    )


def project_far(parts, out_weight, heads, groups, rows, step, tp_size):
    features, columns = out_weight.shape

    def body(parts_ref, weight_ref, attention_ref, far_ref):
        combine(parts_ref, attention_ref, heads, groups, rows)
        far_ref[...] = share_of(attention_ref, weight_ref, step, tp_size).astype(far_ref.dtype)

    return pl.pallas_call(
        body,
        out_shape=(
            jax.ShapeDtypeStruct((rows, features), jnp.bfloat16),
            jax.ShapeDtypeStruct((rows, columns // tp_size), jnp.bfloat16),
        ),
        cost_estimate=pl.CostEstimate(
            flops=2 * rows * features * columns // tp_size,
            bytes_accessed=2 * features * columns,
            transcendentals=0,
        ),
        compiler_params=pltpu.CompilerParams(vmem_limit_bytes=VMEM_LIMIT),
    )(parts, out_weight)


def project_near(attention, out_weight, steps, tp_size):
    rows, features = attention.shape
    columns = out_weight.shape[1]

    def body(attention_ref, weight_ref, *out_refs):
        for step, out_ref in zip(steps, out_refs):
            out_ref[...] = share_of(attention_ref, weight_ref, step, tp_size).astype(
                out_ref.dtype
            )

    return pl.pallas_call(
        body,
        out_shape=[
            jax.ShapeDtypeStruct(
                (rows, columns // tp_size), jnp.bfloat16 if step else jnp.float32
            )
            for step in steps
        ],
        cost_estimate=pl.CostEstimate(
            flops=2 * rows * features * len(steps) * (columns // tp_size),
            bytes_accessed=2 * features * columns,
            transcendentals=0,
        ),
        compiler_params=pltpu.CompilerParams(vmem_limit_bytes=VMEM_LIMIT),
    )(attention, out_weight)


def to_member(share, step, tp_size):
    return lax.ppermute(share, "tp", [(i, (i + step) % tp_size) for i in range(tp_size)])


def shards(queries, keys, values, out_weight):
    rows, features = queries.shape
    heads = features // HEAD_DIM
    groups = lax.axis_size("xb") * lax.axis_size("yl") * lax.axis_size("core")
    tp_size = lax.axis_size("tp")

    one_head = lax.all_to_all(
        pack(queries, keys, values, heads), HEAD_AXES, 0, 0, tiled=True
    ).reshape(heads * rows, 3 * LANES)
    own_kv, sent_q = spread(one_head, groups)
    got_q = lax.all_to_all(sent_q, QUERY_AXES, 0, 0, tiled=True)
    got_kv = lax.all_gather(own_kv, "zh", axis=0, tiled=True)
    partial = attend(got_q.reshape(-1, LANES), got_kv, rows)
    returned = lax.all_to_all(
        partial.reshape(groups * heads, rows, LANES), RETURN_AXES, 0, 0, tiled=True
    )
    far = tp_size // 2
    near = [step for step in range(1, tp_size) if step != far]
    attention, far_share = project_far(
        returned.reshape(-1, LANES), out_weight, heads, groups, rows, far, tp_size
    )
    arrived = [to_member(far_share, far, tp_size)]
    *near_shares, own_share = project_near(attention, out_weight, near + [0], tp_size)
    arrived += [to_member(share, step, tp_size) for share, step in zip(near_shares, near)]
    total = own_share
    for share in arrived:
        total = total + share.astype(jnp.float32)
    return total.astype(jnp.bfloat16)


def solution(mesh):
    split = Mesh(mesh.devices.reshape(2, 2, 2, 4, 2, 2, 4), AXES)
    placed = (P(CTX, "tp"), P(CTX, "tp"), P(CTX, "tp"), P("tp", None))
    return jax.shard_map(
        shards, mesh=split, in_specs=placed, out_specs=P(CTX, "tp"), check_vma=False
    )
```

```python
import math

import jax
import jax.numpy as jnp
from jax import lax
from jax.experimental import pallas as pl
from jax.experimental.pallas import tpu as pltpu
from jax.sharding import Mesh, PartitionSpec as P

HEAD_DIM = 112
LANES = 128
TOTAL, TOTAL_LOW, SHIFT = HEAD_DIM, HEAD_DIM + 1, HEAD_DIM + 2
NEG_FILL = -1e30
NEG_CLAMP = -1e29
AXES = ("xa", "xb", "yl", "zh", "zl", "core", "tp")
CTX = AXES[:6]
HEAD_AXES = ("xa", "zl")
KEY_AXES = ("xb", "yl", "core")
RETURN_AXES = ("zh",) + HEAD_AXES
VMEM_LIMIT = 48 * 1024 * 1024
EXP2_SCALE = math.log2(math.e) / HEAD_DIM**0.5


def pack(queries, keys, values, heads):
    rows = queries.shape[0]
    kind = queries.dtype

    def body(held, out_ref):
        for head in range(heads):
            columns = slice(head * HEAD_DIM, (head + 1) * HEAD_DIM)
            key, value, query = (
                held[part * rows : (part + 1) * rows, columns] for part in range(3)
            )
            gap = jnp.zeros((rows, LANES - HEAD_DIM), kind)
            out_ref[head] = jnp.concatenate(
                [key, gap, value, jnp.ones_like(gap), query, gap], axis=1
            )

    return pl.pallas_call(
        body,
        out_shape=jax.ShapeDtypeStruct((heads, rows, 3 * LANES), kind),
        compiler_params=pltpu.CompilerParams(vmem_limit_bytes=VMEM_LIMIT),
    )(jnp.concatenate([keys, values, queries], axis=0))


def spread(one_head, copies):
    rows = one_head.shape[0]
    kind = one_head.dtype

    def body(one_ref, q_out, kv_out):
        q_out[...] = one_ref[:, 2 * LANES :]
        pair = one_ref[:, : 2 * LANES]
        for copy in range(copies):
            kv_out[copy] = pair

    return pl.pallas_call(
        body,
        out_shape=(
            jax.ShapeDtypeStruct((rows, LANES), kind),
            jax.ShapeDtypeStruct((copies, rows, 2 * LANES), kind),
        ),
        compiler_params=pltpu.CompilerParams(vmem_limit_bytes=VMEM_LIMIT),
    )(one_head)


def attend_kernel(rows, q_ref, kv_ref, out_ref, key_ref, value_ref):
    xb, yl, zh, core = (lax.axis_index(name) for name in ("xb", "yl", "zh", "core"))
    pair = 2 * rows
    block = 2 * pair
    coarse = 4 * block
    sources = kv_ref.shape[0] // block
    half = sources * pair
    for xa_at in range(2):
        for source in range(sources):
            start = source * block + xa_at * pair
            to_rows = slice(xa_at * half + source * pair, xa_at * half + (source + 1) * pair)
            key_ref[to_rows, :] = kv_ref[start : start + pair, :LANES]
            value_ref[to_rows, :] = kv_ref[start : start + pair, LANES:]
    query_at = lax.broadcasted_iota(jnp.int32, (block, half), 0)
    query_at = (query_at // pair) * block + query_at % pair + (query_at // rows % 2) * rows
    key_at = lax.broadcasted_iota(jnp.int32, (block, half), 1)
    source_at = key_at // pair
    key_at = (
        (source_at // 2) * coarse
        + (source_at % 2) * rows
        + key_at % pair
        + (key_at // rows % 2) * rows
    )
    distance = query_at - key_at + (xb * 2 + yl) * coarse + core * rows - zh * block
    lane = lax.broadcasted_iota(jnp.int32, (block, LANES), 1)
    for zh_at in range(0, q_ref.shape[0] // block, 2):
        kept = distance + zh_at * block >= 0
        for xa_at in range(2):
            total = (xa_at + 1) * half
            known = total - half
            starts = [(zh_at + after) * block + xa_at * pair for after in range(2)]
            queries = jnp.concatenate(
                [q_ref[start : start + pair, :] for start in starts], axis=0
            )
            scores = lax.dot_general(
                queries,
                key_ref[:total, :],
                (((1,), (1,)), ((), ())),
                preferred_element_type=jnp.float32,
            )
            last = jnp.where(kept, scores[:, known:], NEG_FILL)
            if known:
                scores = jnp.concatenate([scores[:, :known], last], axis=1)
            else:
                scores = last
            top = jnp.maximum(jnp.max(scores, axis=1, keepdims=True), NEG_CLAMP)
            shift = (top * EXP2_SCALE).astype(jnp.bfloat16).astype(jnp.float32)
            weights = jnp.exp2(scores * EXP2_SCALE - shift)
            weighted = jnp.dot(
                weights.astype(jnp.bfloat16),
                value_ref[:total, :],
                preferred_element_type=jnp.float32,
            )
            rounded = weighted.astype(jnp.bfloat16).astype(jnp.float32)
            weighted = jnp.where(lane == TOTAL_LOW, weighted - rounded, weighted)
            weighted = jnp.where(lane == SHIFT, shift, weighted).astype(out_ref.dtype)
            for after, start in enumerate(starts):
                out_ref[start : start + pair, :] = weighted[after * pair : (after + 1) * pair]


def attend(queries, keys_values, rows):
    def body(*refs):
        attend_kernel(rows, *refs)

    return pl.pallas_call(
        body,
        out_shape=jax.ShapeDtypeStruct(queries.shape, queries.dtype),
        scratch_shapes=[pltpu.VMEM((keys_values.shape[0], LANES), queries.dtype)] * 2,
        compiler_params=pltpu.CompilerParams(vmem_limit_bytes=VMEM_LIMIT),
    )(queries, keys_values)


def combine(parts_ref, attention_ref, heads, groups, rows):
    for head in range(heads):
        parts = [
            parts_ref[
                (group * heads + head) * rows : (group * heads + head + 1) * rows, :
            ].astype(jnp.float32)
            for group in range(groups)
        ]
        shifts = [part[:, SHIFT : SHIFT + 1] for part in parts]
        top = shifts[0]
        for shift in shifts[1:]:
            top = jnp.maximum(top, shift)
        mixed = jnp.zeros_like(parts[0])
        for shift, part in zip(shifts, parts):
            mixed = mixed + jnp.exp2(shift - top) * part
        row_total = mixed[:, TOTAL : TOTAL + 1] + mixed[:, TOTAL_LOW : TOTAL_LOW + 1]
        attention_ref[:, head * HEAD_DIM : (head + 1) * HEAD_DIM] = (
            mixed[:, :HEAD_DIM] / row_total
        ).astype(attention_ref.dtype)


def share_of(attention_ref, weight_ref, step, tp_size):
    width = weight_ref.shape[1] // tp_size
    member = lax.rem(lax.axis_index("tp") + step, tp_size)
    columns = pl.ds(pl.multiple_of(member * width, LANES), width)
    return jnp.dot(
        attention_ref[...], weight_ref[:, columns], preferred_element_type=jnp.float32
    )


def project_far(parts, out_weight, heads, groups, rows, step, tp_size):
    features, columns = out_weight.shape

    def body(parts_ref, weight_ref, attention_ref, far_ref):
        combine(parts_ref, attention_ref, heads, groups, rows)
        far_ref[...] = share_of(attention_ref, weight_ref, step, tp_size).astype(far_ref.dtype)

    return pl.pallas_call(
        body,
        out_shape=(
            jax.ShapeDtypeStruct((rows, features), jnp.bfloat16),
            jax.ShapeDtypeStruct((rows, columns // tp_size), jnp.bfloat16),
        ),
        cost_estimate=pl.CostEstimate(
            flops=2 * rows * features * columns // tp_size,
            bytes_accessed=2 * features * columns,
            transcendentals=0,
        ),
        compiler_params=pltpu.CompilerParams(vmem_limit_bytes=VMEM_LIMIT),
    )(parts, out_weight)


def project_near(attention, out_weight, steps, tp_size):
    rows, features = attention.shape
    columns = out_weight.shape[1]

    def body(attention_ref, weight_ref, *out_refs):
        for step, out_ref in zip(steps, out_refs):
            out_ref[...] = share_of(attention_ref, weight_ref, step, tp_size).astype(
                out_ref.dtype
            )

    return pl.pallas_call(
        body,
        out_shape=[
            jax.ShapeDtypeStruct(
                (rows, columns // tp_size), jnp.bfloat16 if step else jnp.float32
            )
            for step in steps
        ],
        cost_estimate=pl.CostEstimate(
            flops=2 * rows * features * len(steps) * (columns // tp_size),
            bytes_accessed=2 * features * columns,
            transcendentals=0,
        ),
        compiler_params=pltpu.CompilerParams(vmem_limit_bytes=VMEM_LIMIT),
    )(attention, out_weight)


def to_member(share, step, tp_size):
    return lax.ppermute(share, "tp", [(i, (i + step) % tp_size) for i in range(tp_size)])


def shards(queries, keys, values, out_weight):
    rows, features = queries.shape
    heads = features // HEAD_DIM
    groups = lax.axis_size("zh")
    key_copies = lax.axis_size("xb") * lax.axis_size("yl") * lax.axis_size("core")
    tp_size = lax.axis_size("tp")

    one_head = lax.all_to_all(
        pack(queries, keys, values, heads), HEAD_AXES, 0, 0, tiled=True
    ).reshape(heads * rows, 3 * LANES)
    own_q, sent_kv = spread(one_head, key_copies)
    got_kv = lax.all_to_all(sent_kv, KEY_AXES, 0, 0, tiled=True)
    got_q = lax.all_gather(own_q, "zh", axis=0, tiled=True)
    partial = attend(got_q, got_kv.reshape(-1, 2 * LANES), rows)
    returned = lax.all_to_all(
        partial.reshape(groups * heads, rows, LANES), RETURN_AXES, 0, 0, tiled=True
    )
    far = tp_size // 2
    near = [step for step in range(1, tp_size) if step != far]
    attention, far_share = project_far(
        returned.reshape(-1, LANES), out_weight, heads, groups, rows, far, tp_size
    )
    arrived = [to_member(far_share, far, tp_size)]
    *near_shares, own_share = project_near(attention, out_weight, near + [0], tp_size)
    arrived += [to_member(share, step, tp_size) for share, step in zip(near_shares, near)]
    total = own_share
    for share in arrived:
        total = total + share.astype(jnp.float32)
    return total.astype(jnp.bfloat16)


def solution(mesh):
    split = Mesh(mesh.devices.reshape(2, 2, 2, 4, 2, 2, 4), AXES)
    placed = (P(CTX, "tp"), P(CTX, "tp"), P(CTX, "tp"), P("tp", None))
    return jax.shard_map(
        shards, mesh=split, in_specs=placed, out_specs=P(CTX, "tp"), check_vma=False
    )
```

```python
import math

import jax
import jax.numpy as jnp
from jax import lax
from jax.experimental import pallas as pl
from jax.experimental.pallas import tpu as pltpu
from jax.sharding import Mesh, PartitionSpec as P

HEAD_DIM = 112
LANES = 128
TOTAL, TOTAL_LOW, SHIFT = HEAD_DIM, HEAD_DIM + 1, HEAD_DIM + 2
NEG_FILL = -1e30
NEG_CLAMP = -1e29
AXES = ("xa", "xb", "yl", "zh", "zl", "core", "tp")
CTX = AXES[:6]
HEAD_AXES = ("xa", "zl")
KEY_AXES = ("xb", "yl", "core")
RETURN_AXES = ("zh",) + HEAD_AXES
VMEM_LIMIT = 48 * 1024 * 1024
EXP2_SCALE = math.log2(math.e) / HEAD_DIM**0.5


def pack(queries, keys, values, heads):
    rows = queries.shape[0]
    kind = queries.dtype

    def body(held, out_ref):
        for head in range(heads):
            columns = slice(head * HEAD_DIM, (head + 1) * HEAD_DIM)
            key, value, query = (
                held[part * rows : (part + 1) * rows, columns] for part in range(3)
            )
            gap = jnp.zeros((rows, LANES - HEAD_DIM), kind)
            out_ref[head] = jnp.concatenate(
                [key, gap, value, jnp.ones_like(gap), query, gap], axis=1
            )

    return pl.pallas_call(
        body,
        out_shape=jax.ShapeDtypeStruct((heads, rows, 3 * LANES), kind),
        compiler_params=pltpu.CompilerParams(vmem_limit_bytes=VMEM_LIMIT),
    )(jnp.concatenate([keys, values, queries], axis=0))


def spread(one_head, copies):
    rows = one_head.shape[0]
    kind = one_head.dtype

    def body(one_ref, q_out, kv_out):
        q_out[...] = one_ref[:, 2 * LANES :]
        pair = one_ref[:, : 2 * LANES]
        for copy in range(copies):
            kv_out[copy] = pair

    return pl.pallas_call(
        body,
        out_shape=(
            jax.ShapeDtypeStruct((rows, LANES), kind),
            jax.ShapeDtypeStruct((copies, rows, 2 * LANES), kind),
        ),
        compiler_params=pltpu.CompilerParams(vmem_limit_bytes=VMEM_LIMIT),
    )(one_head)


def attend_kernel(rows, q_ref, kv_ref, out_ref, key_ref, value_ref):
    xb, yl, zh, core = (lax.axis_index(name) for name in ("xb", "yl", "zh", "core"))
    pair = 2 * rows
    block = 2 * pair
    coarse = 4 * block
    sources = kv_ref.shape[0] // block
    half = sources * pair
    for xa_at in range(2):
        for source in range(sources):
            start = source * block + xa_at * pair
            to_rows = slice(xa_at * half + source * pair, xa_at * half + (source + 1) * pair)
            key_ref[to_rows, :] = kv_ref[start : start + pair, :LANES]
            value_ref[to_rows, :] = kv_ref[start : start + pair, LANES:]
    query_at = lax.broadcasted_iota(jnp.int32, (block, half), 0)
    query_at = (query_at // pair) * block + query_at % pair + (query_at // rows % 2) * rows
    key_at = lax.broadcasted_iota(jnp.int32, (block, half), 1)
    source_at = key_at // pair
    key_at = (
        (source_at // 2) * coarse
        + (source_at % 2) * rows
        + key_at % pair
        + (key_at // rows % 2) * rows
    )
    distance = query_at - key_at + (xb * 2 + yl) * coarse + core * rows - zh * block
    lane = lax.broadcasted_iota(jnp.int32, (block, LANES), 1)
    for zh_at in range(0, q_ref.shape[0] // block, 2):
        kept = distance + zh_at * block >= 0
        for xa_at in range(2):
            total = (xa_at + 1) * half
            known = total - half
            starts = [(zh_at + after) * block + xa_at * pair for after in range(2)]
            queries = jnp.concatenate(
                [q_ref[start : start + pair, :] for start in starts], axis=0
            )
            scores = lax.dot_general(
                queries,
                key_ref[:total, :],
                (((1,), (1,)), ((), ())),
                preferred_element_type=jnp.float32,
            )
            last = jnp.where(kept, scores[:, known:], NEG_FILL)
            if known:
                scores = jnp.concatenate([scores[:, :known], last], axis=1)
            else:
                scores = last
            top = jnp.maximum(jnp.max(scores, axis=1, keepdims=True), NEG_CLAMP)
            shift = (top * EXP2_SCALE).astype(jnp.bfloat16).astype(jnp.float32)
            weights = jnp.exp2(scores * EXP2_SCALE - shift)
            weighted = jnp.dot(
                weights.astype(jnp.bfloat16),
                value_ref[:total, :],
                preferred_element_type=jnp.float32,
            )
            rounded = weighted.astype(jnp.bfloat16).astype(jnp.float32)
            weighted = jnp.where(lane == TOTAL_LOW, weighted - rounded, weighted)
            weighted = jnp.where(lane == SHIFT, shift, weighted).astype(out_ref.dtype)
            for after, start in enumerate(starts):
                out_ref[start : start + pair, :] = weighted[after * pair : (after + 1) * pair]


def attend(queries, keys_values, rows):
    def body(*refs):
        attend_kernel(rows, *refs)

    return pl.pallas_call(
        body,
        out_shape=jax.ShapeDtypeStruct(queries.shape, queries.dtype),
        scratch_shapes=[pltpu.VMEM((keys_values.shape[0], LANES), queries.dtype)] * 2,
        compiler_params=pltpu.CompilerParams(vmem_limit_bytes=VMEM_LIMIT),
    )(queries, keys_values)


def combine(parts_ref, attention_ref, heads, groups, rows):
    for head in range(heads):
        parts = [
            parts_ref[
                (group * heads + head) * rows : (group * heads + head + 1) * rows, :
            ].astype(jnp.float32)
            for group in range(groups)
        ]
        shifts = [part[:, SHIFT : SHIFT + 1] for part in parts]
        top = shifts[0]
        for shift in shifts[1:]:
            top = jnp.maximum(top, shift)
        mixed = jnp.zeros_like(parts[0])
        for shift, part in zip(shifts, parts):
            mixed = mixed + jnp.exp2(shift - top) * part
        row_total = mixed[:, TOTAL : TOTAL + 1] + mixed[:, TOTAL_LOW : TOTAL_LOW + 1]
        attention_ref[:, head * HEAD_DIM : (head + 1) * HEAD_DIM] = (
            mixed[:, :HEAD_DIM] / row_total
        ).astype(attention_ref.dtype)


def share_of(attention_ref, weight_ref, step, tp_size):
    width = weight_ref.shape[1] // tp_size
    member = lax.rem(lax.axis_index("tp") + step, tp_size)
    columns = pl.ds(pl.multiple_of(member * width, LANES), width)
    return jnp.dot(
        attention_ref[...], weight_ref[:, columns], preferred_element_type=jnp.float32
    )


def project_first(parts, out_weight, heads, groups, rows, steps, tp_size):
    features, columns = out_weight.shape
    width = columns // tp_size

    def body(parts_ref, weight_ref, attention_ref, *out_refs):
        combine(parts_ref, attention_ref, heads, groups, rows)
        for step, out_ref in zip(steps, out_refs):
            out_ref[...] = share_of(attention_ref, weight_ref, step, tp_size).astype(
                out_ref.dtype
            )

    return pl.pallas_call(
        body,
        out_shape=[jax.ShapeDtypeStruct((rows, features), jnp.bfloat16)]
        + [jax.ShapeDtypeStruct((rows, width), jnp.bfloat16) for _ in steps],
        cost_estimate=pl.CostEstimate(
            flops=2 * rows * features * width * len(steps),
            bytes_accessed=2 * features * columns,
            transcendentals=0,
        ),
        compiler_params=pltpu.CompilerParams(vmem_limit_bytes=VMEM_LIMIT),
    )(parts, out_weight)


def project_rest(attention, out_weight, steps, tp_size):
    rows, features = attention.shape
    columns = out_weight.shape[1]

    def body(attention_ref, weight_ref, *out_refs):
        for step, out_ref in zip(steps, out_refs):
            out_ref[...] = share_of(attention_ref, weight_ref, step, tp_size).astype(
                out_ref.dtype
            )

    return pl.pallas_call(
        body,
        out_shape=[
            jax.ShapeDtypeStruct(
                (rows, columns // tp_size), jnp.bfloat16 if step else jnp.float32
            )
            for step in steps
        ],
        cost_estimate=pl.CostEstimate(
            flops=2 * rows * features * len(steps) * (columns // tp_size),
            bytes_accessed=2 * features * columns,
            transcendentals=0,
        ),
        compiler_params=pltpu.CompilerParams(vmem_limit_bytes=VMEM_LIMIT),
    )(attention, out_weight)


def to_member(share, step, tp_size):
    return lax.ppermute(share, "tp", [(i, (i + step) % tp_size) for i in range(tp_size)])


def shards(queries, keys, values, out_weight):
    rows, features = queries.shape
    heads = features // HEAD_DIM
    groups = lax.axis_size("zh")
    key_copies = lax.axis_size("xb") * lax.axis_size("yl") * lax.axis_size("core")
    tp_size = lax.axis_size("tp")

    one_head = lax.all_to_all(
        pack(queries, keys, values, heads), HEAD_AXES, 0, 0, tiled=True
    ).reshape(heads * rows, 3 * LANES)
    own_q, sent_kv = spread(one_head, key_copies)
    got_kv = lax.all_to_all(sent_kv, KEY_AXES, 0, 0, tiled=True)
    got_q = lax.all_gather(own_q, "zh", axis=0, tiled=True)
    partial = attend(got_q, got_kv.reshape(-1, 2 * LANES), rows)
    returned = lax.all_to_all(
        partial.reshape(groups * heads, rows, LANES), RETURN_AXES, 0, 0, tiled=True
    )
    far = tp_size // 2
    near = [step for step in range(1, tp_size) if step != far]
    attention, *near_shares = project_first(
        returned.reshape(-1, LANES), out_weight, heads, groups, rows, near, tp_size
    )
    arrived = [to_member(share, step, tp_size) for share, step in zip(near_shares, near)]
    far_share, own_share = project_rest(attention, out_weight, [far, 0], tp_size)
    arrived.append(to_member(far_share, far, tp_size))
    total = own_share
    for share in arrived:
        total = total + share.astype(jnp.float32)
    return total.astype(jnp.bfloat16)


def solution(mesh):
    split = Mesh(mesh.devices.reshape(2, 2, 2, 4, 2, 2, 4), AXES)
    placed = (P(CTX, "tp"), P(CTX, "tp"), P(CTX, "tp"), P("tp", None))
    return jax.shard_map(
        shards, mesh=split, in_specs=placed, out_specs=P(CTX, "tp"), check_vma=False
    )
```

```python
import math

import jax
import jax.numpy as jnp
from jax import lax
from jax.experimental import pallas as pl
from jax.experimental.pallas import tpu as pltpu
from jax.sharding import Mesh, PartitionSpec as P

HEAD_DIM = 112
LANES = 128
ZH_STEP = 2
TOTAL, TOTAL_LOW, SHIFT = HEAD_DIM, HEAD_DIM + 1, HEAD_DIM + 2
NEG_FILL = -1e30
NEG_CLAMP = -1e29
AXES = ("xa", "xb", "yl", "zh", "zl", "core", "tp")
CTX = AXES[:6]
HEAD_AXES = ("xa", "zl")
KEY_AXES = ("xb", "yl", "core")
RETURN_AXES = ("zh",) + HEAD_AXES
VMEM_LIMIT = 48 * 1024 * 1024
EXP2_SCALE = math.log2(math.e) / HEAD_DIM**0.5


def pack(queries, keys, values, heads):
    rows = queries.shape[0]
    kind = queries.dtype

    def body(held, out_ref):
        for head in range(heads):
            columns = slice(head * HEAD_DIM, (head + 1) * HEAD_DIM)
            key, value, query = (
                held[part * rows : (part + 1) * rows, columns] for part in range(3)
            )
            gap = jnp.zeros((rows, LANES - HEAD_DIM), kind)
            out_ref[head] = jnp.concatenate(
                [key, gap, value, jnp.ones_like(gap), query, gap], axis=1
            )

    return pl.pallas_call(
        body,
        out_shape=jax.ShapeDtypeStruct((heads, rows, 3 * LANES), kind),
        compiler_params=pltpu.CompilerParams(vmem_limit_bytes=VMEM_LIMIT),
    )(jnp.concatenate([keys, values, queries], axis=0))


def spread(one_head, copies):
    rows = one_head.shape[0]
    kind = one_head.dtype

    def body(one_ref, q_out, kv_out):
        q_out[...] = one_ref[:, 2 * LANES :]
        pair = one_ref[:, : 2 * LANES]
        for copy in range(copies):
            kv_out[copy] = pair

    return pl.pallas_call(
        body,
        out_shape=(
            jax.ShapeDtypeStruct((rows, LANES), kind),
            jax.ShapeDtypeStruct((copies, rows, 2 * LANES), kind),
        ),
        compiler_params=pltpu.CompilerParams(vmem_limit_bytes=VMEM_LIMIT),
    )(one_head)


def attend_kernel(rows, zh_step, q_ref, kv_hbm, out_ref, kv_ref, arrived):
    xb, yl, zh, core = (lax.axis_index(name) for name in ("xb", "yl", "zh", "core"))
    pair = 2 * rows
    block = 2 * pair
    coarse = 4 * block
    zh_size = q_ref.shape[0]
    sources = kv_hbm.shape[0]
    half = sources * pair
    loads = [
        pltpu.make_async_copy(
            kv_hbm.at[:, xa_at * pair : (xa_at + 1) * pair, :],
            kv_ref.at[xa_at],
            arrived.at[xa_at],
        )
        for xa_at in range(2)
    ]
    for load in loads:
        load.start()
    tile = zh_step * pair
    query_at = lax.broadcasted_iota(jnp.int32, (tile, half), 0)
    query_at = (query_at // pair) * block + query_at % pair + (query_at // rows % 2) * rows
    key_at = lax.broadcasted_iota(jnp.int32, (tile, half), 1)
    source_at = key_at // pair
    key_at = (
        (source_at // 2) * coarse
        + (source_at % 2) * rows
        + key_at % pair
        + (key_at // rows % 2) * rows
    )
    distance = query_at - key_at + (xb * 2 + yl) * coarse + core * rows - zh * block
    lane = lax.broadcasted_iota(jnp.int32, (tile, LANES), 1)
    for xa_at in range(2):
        loads[xa_at].wait()
        keys = [kv_ref[at, :, :, :LANES].reshape(half, LANES) for at in range(xa_at + 1)]
        values = [kv_ref[at, :, :, LANES:].reshape(half, LANES) for at in range(xa_at + 1)]
        for zh_at in range(0, zh_size, zh_step):
            own = (slice(zh_at, zh_at + zh_step), slice(xa_at * pair, (xa_at + 1) * pair))
            queries = q_ref[own].reshape(tile, LANES)
            scores = [
                lax.dot_general(
                    queries, key, (((1,), (1,)), ((), ())), preferred_element_type=jnp.float32
                )
                for key in keys
            ]
            scores[-1] = jnp.where(distance + zh_at * block >= 0, scores[-1], NEG_FILL)
            top = jnp.max(scores[0], axis=1, keepdims=True)
            for score in scores[1:]:
                top = jnp.maximum(top, jnp.max(score, axis=1, keepdims=True))
            top = jnp.maximum(top, NEG_CLAMP)
            shift = (top * EXP2_SCALE).astype(jnp.bfloat16).astype(jnp.float32)
            weighted = jnp.zeros((tile, LANES), jnp.float32)
            for score, value in zip(scores, values):
                weights = jnp.exp2(score * EXP2_SCALE - shift).astype(jnp.bfloat16)
                weighted = weighted + jnp.dot(
                    weights, value, preferred_element_type=jnp.float32
                )
            rounded = weighted.astype(jnp.bfloat16).astype(jnp.float32)
            weighted = jnp.where(lane == TOTAL_LOW, weighted - rounded, weighted)
            weighted = jnp.where(lane == SHIFT, shift, weighted).astype(out_ref.dtype)
            out_ref[own] = weighted.reshape(zh_step, pair, LANES)


def attend(queries, keys_values, rows, zh_step):
    sources, block, width = keys_values.shape

    def body(*refs):
        attend_kernel(rows, zh_step, *refs)

    return pl.pallas_call(
        body,
        in_specs=[pl.BlockSpec(memory_space=pltpu.VMEM), pl.BlockSpec(memory_space=pl.ANY)],
        out_shape=jax.ShapeDtypeStruct(queries.shape, queries.dtype),
        scratch_shapes=[
            pltpu.VMEM((2, sources, block // 2, width), queries.dtype),
            pltpu.SemaphoreType.DMA((2,)),
        ],
        compiler_params=pltpu.CompilerParams(vmem_limit_bytes=VMEM_LIMIT),
    )(queries, keys_values)


def combine(parts_ref, attention_ref, heads, groups, rows):
    for head in range(heads):
        parts = [
            parts_ref[
                (group * heads + head) * rows : (group * heads + head + 1) * rows, :
            ].astype(jnp.float32)
            for group in range(groups)
        ]
        shifts = [part[:, SHIFT : SHIFT + 1] for part in parts]
        top = shifts[0]
        for shift in shifts[1:]:
            top = jnp.maximum(top, shift)
        mixed = jnp.zeros_like(parts[0])
        for shift, part in zip(shifts, parts):
            mixed = mixed + jnp.exp2(shift - top) * part
        row_total = mixed[:, TOTAL : TOTAL + 1] + mixed[:, TOTAL_LOW : TOTAL_LOW + 1]
        attention_ref[:, head * HEAD_DIM : (head + 1) * HEAD_DIM] = (
            mixed[:, :HEAD_DIM] / row_total
        ).astype(attention_ref.dtype)


def share_of(attention_ref, weight_ref, step, tp_size):
    width = weight_ref.shape[1] // tp_size
    member = lax.rem(lax.axis_index("tp") + step, tp_size)
    columns = pl.ds(pl.multiple_of(member * width, LANES), width)
    return jnp.dot(
        attention_ref[...], weight_ref[:, columns], preferred_element_type=jnp.float32
    )


def project_far(parts, out_weight, heads, groups, rows, step, tp_size):
    features, columns = out_weight.shape

    def body(parts_ref, weight_ref, attention_ref, far_ref):
        combine(parts_ref, attention_ref, heads, groups, rows)
        far_ref[...] = share_of(attention_ref, weight_ref, step, tp_size).astype(far_ref.dtype)

    return pl.pallas_call(
        body,
        out_shape=(
            jax.ShapeDtypeStruct((rows, features), jnp.bfloat16),
            jax.ShapeDtypeStruct((rows, columns // tp_size), jnp.bfloat16),
        ),
        cost_estimate=pl.CostEstimate(
            flops=2 * rows * features * columns // tp_size,
            bytes_accessed=2 * features * columns,
            transcendentals=0,
        ),
        compiler_params=pltpu.CompilerParams(vmem_limit_bytes=VMEM_LIMIT),
    )(parts, out_weight)


def project_near(attention, out_weight, steps, tp_size):
    rows, features = attention.shape
    columns = out_weight.shape[1]

    def body(attention_ref, weight_ref, *out_refs):
        for step, out_ref in zip(steps, out_refs):
            out_ref[...] = share_of(attention_ref, weight_ref, step, tp_size).astype(
                out_ref.dtype
            )

    return pl.pallas_call(
        body,
        out_shape=[
            jax.ShapeDtypeStruct(
                (rows, columns // tp_size), jnp.bfloat16 if step else jnp.float32
            )
            for step in steps
        ],
        cost_estimate=pl.CostEstimate(
            flops=2 * rows * features * len(steps) * (columns // tp_size),
            bytes_accessed=2 * features * columns,
            transcendentals=0,
        ),
        compiler_params=pltpu.CompilerParams(vmem_limit_bytes=VMEM_LIMIT),
    )(attention, out_weight)


def to_member(share, step, tp_size):
    return lax.ppermute(share, "tp", [(i, (i + step) % tp_size) for i in range(tp_size)])


def shards(queries, keys, values, out_weight):
    rows, features = queries.shape
    heads = features // HEAD_DIM
    groups = lax.axis_size("zh")
    key_copies = lax.axis_size("xb") * lax.axis_size("yl") * lax.axis_size("core")
    tp_size = lax.axis_size("tp")

    one_head = lax.all_to_all(
        pack(queries, keys, values, heads), HEAD_AXES, 0, 0, tiled=True
    ).reshape(heads * rows, 3 * LANES)
    own_q, sent_kv = spread(one_head, key_copies)
    got_kv = lax.all_to_all(sent_kv, KEY_AXES, 0, 0, tiled=True)
    got_q = lax.all_gather(own_q, "zh", axis=0, tiled=True)
    got_q = got_q.reshape(groups, heads * rows, LANES)
    partial = attend(got_q, got_kv, rows, ZH_STEP)
    returned = lax.all_to_all(
        partial.reshape(groups * heads, rows, LANES), RETURN_AXES, 0, 0, tiled=True
    )
    far = tp_size // 2
    near = [step for step in range(1, tp_size) if step != far]
    attention, far_share = project_far(
        returned.reshape(-1, LANES), out_weight, heads, groups, rows, far, tp_size
    )
    arrived = [to_member(far_share, far, tp_size)]
    *near_shares, own_share = project_near(attention, out_weight, near + [0], tp_size)
    arrived += [to_member(share, step, tp_size) for share, step in zip(near_shares, near)]
    total = own_share
    for share in arrived:
        total = total + share.astype(jnp.float32)
    return total.astype(jnp.bfloat16)


def solution(mesh):
    split = Mesh(mesh.devices.reshape(2, 2, 2, 4, 2, 2, 4), AXES)
    placed = (P(CTX, "tp"), P(CTX, "tp"), P(CTX, "tp"), P("tp", None))
    return jax.shard_map(
        shards, mesh=split, in_specs=placed, out_specs=P(CTX, "tp"), check_vma=False
    )
```

```python
import math

import jax
import jax.numpy as jnp
from jax import lax
from jax.experimental import pallas as pl
from jax.experimental.pallas import tpu as pltpu
from jax.sharding import Mesh, PartitionSpec as P

HEAD_DIM = 112
LANES = 128
TOTAL, TOTAL_LOW, SHIFT = HEAD_DIM, HEAD_DIM + 1, HEAD_DIM + 2
NEG_FILL = -1e30
NEG_CLAMP = -1e29
AXES = ("xa", "xb", "yl", "zh", "zl", "core", "tp")
CTX = AXES[:6]
HEAD_AXES = ("xa", "zl")
KEY_AXES = ("xb", "yl", "core")
RETURN_AXES = ("zh",) + HEAD_AXES
VMEM_LIMIT = 48 * 1024 * 1024
EXP2_SCALE = math.log2(math.e) / HEAD_DIM**0.5


def pack(queries, keys, values, heads):
    rows = queries.shape[0]
    kind = queries.dtype

    def body(held, out_ref):
        for head in range(heads):
            columns = slice(head * HEAD_DIM, (head + 1) * HEAD_DIM)
            key, value, query = (
                held[part * rows : (part + 1) * rows, columns] for part in range(3)
            )
            gap = jnp.zeros((rows, LANES - HEAD_DIM), kind)
            out_ref[head] = jnp.concatenate(
                [key, gap, value, jnp.ones_like(gap), query, gap], axis=1
            )

    return pl.pallas_call(
        body,
        out_shape=jax.ShapeDtypeStruct((heads, rows, 3 * LANES), kind),
        compiler_params=pltpu.CompilerParams(vmem_limit_bytes=VMEM_LIMIT),
    )(jnp.concatenate([keys, values, queries], axis=0))


def spread(one_head, copies):
    rows = one_head.shape[0]
    kind = one_head.dtype

    def body(one_ref, q_out, kv_out):
        q_out[...] = one_ref[:, 2 * LANES :]
        pair = one_ref[:, : 2 * LANES]
        for copy in range(copies):
            kv_out[copy] = pair

    return pl.pallas_call(
        body,
        out_shape=(
            jax.ShapeDtypeStruct((rows, LANES), kind),
            jax.ShapeDtypeStruct((copies, rows, 2 * LANES), kind),
        ),
        compiler_params=pltpu.CompilerParams(vmem_limit_bytes=VMEM_LIMIT),
    )(one_head)


def attend_kernel(rows, q_ref, kv_ref, out_ref, key_ref, value_ref):
    xb, yl, zh, core = (lax.axis_index(name) for name in ("xb", "yl", "zh", "core"))
    pair = 2 * rows
    block = 2 * pair
    coarse = 4 * block
    sources = kv_ref.shape[0] // block
    half = sources * pair
    for xa_at in range(2):
        for source in range(sources):
            start = source * block + xa_at * pair
            to_rows = slice(xa_at * half + source * pair, xa_at * half + (source + 1) * pair)
            key_ref[to_rows, :] = kv_ref[start : start + pair, :LANES]
            value_ref[to_rows, :] = kv_ref[start : start + pair, LANES:]
    query_at = lax.broadcasted_iota(jnp.int32, (block, half), 0)
    query_at = (query_at // pair) * block + query_at % pair + (query_at // rows % 2) * rows
    key_at = lax.broadcasted_iota(jnp.int32, (block, half), 1)
    source_at = key_at // pair
    key_at = (
        (source_at // 2) * coarse
        + (source_at % 2) * rows
        + key_at % pair
        + (key_at // rows % 2) * rows
    )
    distance = query_at - key_at + (xb * 2 + yl) * coarse + core * rows - zh * block
    lane = lax.broadcasted_iota(jnp.int32, (block, LANES), 1)
    for zh_at in range(0, q_ref.shape[0] // block, 2):
        kept = distance + zh_at * block >= 0
        for xa_at in range(2):
            total = (xa_at + 1) * half
            known = total - half
            starts = [(zh_at + after) * block + xa_at * pair for after in range(2)]
            queries = jnp.concatenate(
                [q_ref[start : start + pair, :] for start in starts], axis=0
            )
            scores = lax.dot_general(
                queries,
                key_ref[:total, :],
                (((1,), (1,)), ((), ())),
                preferred_element_type=jnp.float32,
            )
            last = jnp.where(kept, scores[:, known:], NEG_FILL)
            if known:
                scores = jnp.concatenate([scores[:, :known], last], axis=1)
            else:
                scores = last
            top = jnp.maximum(jnp.max(scores, axis=1, keepdims=True), NEG_CLAMP)
            shift = (top * EXP2_SCALE).astype(jnp.bfloat16).astype(jnp.float32)
            weights = jnp.exp2(scores * EXP2_SCALE - shift)
            weighted = jnp.dot(
                weights.astype(jnp.bfloat16),
                value_ref[:total, :],
                preferred_element_type=jnp.float32,
            )
            rounded = weighted.astype(jnp.bfloat16).astype(jnp.float32)
            weighted = jnp.where(lane == TOTAL_LOW, weighted - rounded, weighted)
            weighted = jnp.where(lane == SHIFT, shift, weighted).astype(out_ref.dtype)
            for after, start in enumerate(starts):
                out_ref[start : start + pair, :] = weighted[after * pair : (after + 1) * pair]


def attend(queries, keys_values, rows):
    def body(*refs):
        attend_kernel(rows, *refs)

    return pl.pallas_call(
        body,
        out_shape=jax.ShapeDtypeStruct(queries.shape, queries.dtype),
        scratch_shapes=[pltpu.VMEM((keys_values.shape[0], LANES), queries.dtype)] * 2,
        compiler_params=pltpu.CompilerParams(vmem_limit_bytes=VMEM_LIMIT),
    )(queries, keys_values)


def combine(parts_ref, attention_ref, heads, groups, rows):
    for head in range(heads):
        parts = [
            parts_ref[
                (group * heads + head) * rows : (group * heads + head + 1) * rows, :
            ].astype(jnp.float32)
            for group in range(groups)
        ]
        shifts = [part[:, SHIFT : SHIFT + 1] for part in parts]
        top = shifts[0]
        for shift in shifts[1:]:
            top = jnp.maximum(top, shift)
        mixed = jnp.zeros_like(parts[0])
        for shift, part in zip(shifts, parts):
            mixed = mixed + jnp.exp2(shift - top) * part
        row_total = mixed[:, TOTAL : TOTAL + 1] + mixed[:, TOTAL_LOW : TOTAL_LOW + 1]
        attention_ref[:, head * HEAD_DIM : (head + 1) * HEAD_DIM] = (
            mixed[:, :HEAD_DIM] / row_total
        ).astype(attention_ref.dtype)


def share_of(attention_ref, weight_ref, step, tp_size):
    width = weight_ref.shape[1] // tp_size
    member = lax.rem(lax.axis_index("tp") + step, tp_size)
    columns = pl.ds(pl.multiple_of(member * width, LANES), width)
    return jnp.dot(
        attention_ref[...], weight_ref[:, columns], preferred_element_type=jnp.float32
    )


def project_far(parts, out_weight, heads, groups, rows, step, tp_size):
    features, columns = out_weight.shape

    def body(parts_ref, weight_ref, attention_ref, far_ref):
        combine(parts_ref, attention_ref, heads, groups, rows)
        far_ref[...] = share_of(attention_ref, weight_ref, step, tp_size).astype(far_ref.dtype)

    return pl.pallas_call(
        body,
        out_shape=(
            jax.ShapeDtypeStruct((rows, features), jnp.bfloat16),
            jax.ShapeDtypeStruct((rows, columns // tp_size), jnp.bfloat16),
        ),
        cost_estimate=pl.CostEstimate(
            flops=2 * rows * features * columns // tp_size,
            bytes_accessed=2 * features * columns,
            transcendentals=0,
        ),
        compiler_params=pltpu.CompilerParams(vmem_limit_bytes=VMEM_LIMIT),
    )(parts, out_weight)


def project_near(attention, out_weight, steps, tp_size):
    rows, features = attention.shape
    columns = out_weight.shape[1]

    def body(attention_ref, weight_ref, *out_refs):
        for step, out_ref in zip(steps, out_refs):
            out_ref[...] = share_of(attention_ref, weight_ref, step, tp_size).astype(
                out_ref.dtype
            )

    return pl.pallas_call(
        body,
        out_shape=[
            jax.ShapeDtypeStruct(
                (rows, columns // tp_size), jnp.bfloat16 if step else jnp.float32
            )
            for step in steps
        ],
        cost_estimate=pl.CostEstimate(
            flops=2 * rows * features * len(steps) * (columns // tp_size),
            bytes_accessed=2 * features * columns,
            transcendentals=0,
        ),
        compiler_params=pltpu.CompilerParams(vmem_limit_bytes=VMEM_LIMIT),
    )(attention, out_weight)


def to_member(share, step, tp_size):
    return lax.ppermute(share, "tp", [(i, (i + step) % tp_size) for i in range(tp_size)])


def shards(queries, keys, values, out_weight):
    rows, features = queries.shape
    heads = features // HEAD_DIM
    groups = lax.axis_size("zh")
    key_copies = lax.axis_size("xb") * lax.axis_size("yl") * lax.axis_size("core")
    tp_size = lax.axis_size("tp")

    one_head = lax.all_to_all(
        pack(queries, keys, values, heads), HEAD_AXES, 0, 0, tiled=True
    ).reshape(heads * rows, 3 * LANES)
    own_q, sent_kv = spread(one_head, key_copies)
    got_kv = lax.all_to_all(sent_kv, KEY_AXES, 0, 0, tiled=True)
    got_q = lax.all_gather(own_q, "zh", axis=0, tiled=True)
    partial = attend(got_q, got_kv.reshape(-1, 2 * LANES), rows)
    returned = lax.all_to_all(
        partial.reshape(groups * heads, rows, LANES), RETURN_AXES, 0, 0, tiled=True
    )
    far = tp_size // 2
    near = [step for step in range(tp_size - 1, 0, -1) if step != far]
    attention, far_share = project_far(
        returned.reshape(-1, LANES), out_weight, heads, groups, rows, far, tp_size
    )
    arrived = [to_member(far_share, far, tp_size)]
    *near_shares, own_share = project_near(attention, out_weight, near + [0], tp_size)
    arrived += [to_member(share, step, tp_size) for share, step in zip(near_shares, near)]
    total = own_share
    for share in arrived:
        total = total + share.astype(jnp.float32)
    return total.astype(jnp.bfloat16)


def solution(mesh):
    split = Mesh(mesh.devices.reshape(2, 2, 2, 4, 2, 2, 4), AXES)
    placed = (P(CTX, "tp"), P(CTX, "tp"), P(CTX, "tp"), P("tp", None))
    return jax.shard_map(
        shards, mesh=split, in_specs=placed, out_specs=P(CTX, "tp"), check_vma=False
    )
```

```python
import math

import jax
import jax.numpy as jnp
from jax import lax
from jax.experimental import pallas as pl
from jax.experimental.pallas import tpu as pltpu
from jax.sharding import Mesh, PartitionSpec as P

HEAD_DIM = 112
LANES = 128
TOTAL, TOTAL_LOW, SHIFT = HEAD_DIM, HEAD_DIM + 1, HEAD_DIM + 2
NEG_FILL = -1e30
NEG_CLAMP = -1e29
AXES = ("xa", "xb", "yl", "zh", "zl", "core", "tp")
CTX = AXES[:6]
HEAD_AXES = ("xa", "zl")
KEY_AXES = ("xb", "yl", "core")
RETURN_AXES = ("xa", "zh", "zl")
VMEM_LIMIT = 48 * 1024 * 1024
EXP2_SCALE = math.log2(math.e) / HEAD_DIM**0.5


def pack(queries, keys, values, heads):
    rows = queries.shape[0]
    kind = queries.dtype

    def body(held, out_ref):
        for head in range(heads):
            columns = slice(head * HEAD_DIM, (head + 1) * HEAD_DIM)
            key, value, query = (
                held[part * rows : (part + 1) * rows, columns] for part in range(3)
            )
            gap = jnp.zeros((rows, LANES - HEAD_DIM), kind)
            out_ref[head] = jnp.concatenate(
                [key, gap, value, jnp.ones_like(gap), query, gap], axis=1
            )

    return pl.pallas_call(
        body,
        out_shape=jax.ShapeDtypeStruct((heads, rows, 3 * LANES), kind),
        compiler_params=pltpu.CompilerParams(vmem_limit_bytes=VMEM_LIMIT),
    )(jnp.concatenate([keys, values, queries], axis=0))


def spread(one_head, copies):
    rows = one_head.shape[0]
    kind = one_head.dtype

    def body(one_ref, q_out, kv_out):
        q_out[...] = one_ref[:, 2 * LANES :]
        pair = one_ref[:, : 2 * LANES]
        for copy in range(copies):
            kv_out[copy] = pair

    return pl.pallas_call(
        body,
        out_shape=(
            jax.ShapeDtypeStruct((rows, LANES), kind),
            jax.ShapeDtypeStruct((copies, rows, 2 * LANES), kind),
        ),
        compiler_params=pltpu.CompilerParams(vmem_limit_bytes=VMEM_LIMIT),
    )(one_head)


def attend_kernel(rows, q_ref, kv_ref, out_ref, key_ref, value_ref):
    xb, yl, zh, core = (lax.axis_index(name) for name in ("xb", "yl", "zh", "core"))
    pair = 2 * rows
    block = 2 * pair
    coarse = 4 * block
    sources = kv_ref.shape[0] // block
    half = sources * pair
    for xa_at in range(2):
        for source in range(sources):
            start = source * block + xa_at * pair
            to_rows = slice(xa_at * half + source * pair, xa_at * half + (source + 1) * pair)
            key_ref[to_rows, :] = kv_ref[start : start + pair, :LANES]
            value_ref[to_rows, :] = kv_ref[start : start + pair, LANES:]
    query_at = lax.broadcasted_iota(jnp.int32, (block, half), 0)
    query_at = (query_at // pair) * block + query_at % pair + (query_at // rows % 2) * rows
    key_at = lax.broadcasted_iota(jnp.int32, (block, half), 1)
    source_at = key_at // pair
    key_at = (
        (source_at // 2) * coarse
        + (source_at % 2) * rows
        + key_at % pair
        + (key_at // rows % 2) * rows
    )
    distance = query_at - key_at + (xb * 2 + yl) * coarse + core * rows - zh * block
    lane = lax.broadcasted_iota(jnp.int32, (block, LANES), 1)
    for zh_at in range(0, q_ref.shape[0] // block, 2):
        kept = distance + zh_at * block >= 0
        for xa_at in range(2):
            total = (xa_at + 1) * half
            known = total - half
            starts = [(zh_at + after) * block + xa_at * pair for after in range(2)]
            queries = jnp.concatenate(
                [q_ref[start : start + pair, :] for start in starts], axis=0
            )
            scores = lax.dot_general(
                queries,
                key_ref[:total, :],
                (((1,), (1,)), ((), ())),
                preferred_element_type=jnp.float32,
            )
            last = jnp.where(kept, scores[:, known:], NEG_FILL)
            if known:
                scores = jnp.concatenate([scores[:, :known], last], axis=1)
            else:
                scores = last
            top = jnp.maximum(jnp.max(scores, axis=1, keepdims=True), NEG_CLAMP)
            shift = (top * EXP2_SCALE).astype(jnp.bfloat16).astype(jnp.float32)
            weights = jnp.exp2(scores * EXP2_SCALE - shift)
            weighted = jnp.dot(
                weights.astype(jnp.bfloat16),
                value_ref[:total, :],
                preferred_element_type=jnp.float32,
            )
            rounded = weighted.astype(jnp.bfloat16).astype(jnp.float32)
            weighted = jnp.where(lane == TOTAL_LOW, weighted - rounded, weighted)
            weighted = jnp.where(lane == SHIFT, shift, weighted).astype(out_ref.dtype)
            start = xa_at * (q_ref.shape[0] // 2) + zh_at * pair
            out_ref[start : start + block, :] = weighted


def attend(queries, keys_values, rows):
    def body(*refs):
        attend_kernel(rows, *refs)

    return pl.pallas_call(
        body,
        out_shape=jax.ShapeDtypeStruct(queries.shape, queries.dtype),
        scratch_shapes=[pltpu.VMEM((keys_values.shape[0], LANES), queries.dtype)] * 2,
        compiler_params=pltpu.CompilerParams(vmem_limit_bytes=VMEM_LIMIT),
    )(queries, keys_values)


def combine(parts_ref, attention_ref, heads, groups, rows):
    for head in range(heads):
        parts = [
            parts_ref[at * rows : (at + 1) * rows, :].astype(jnp.float32)
            for at in range(head // 2 * 2 * groups + head % 2, (head // 2 + 1) * 2 * groups, 2)
        ]
        shifts = [part[:, SHIFT : SHIFT + 1] for part in parts]
        top = shifts[0]
        for shift in shifts[1:]:
            top = jnp.maximum(top, shift)
        mixed = jnp.zeros_like(parts[0])
        for shift, part in zip(shifts, parts):
            mixed = mixed + jnp.exp2(shift - top) * part
        row_total = mixed[:, TOTAL : TOTAL + 1] + mixed[:, TOTAL_LOW : TOTAL_LOW + 1]
        attention_ref[:, head * HEAD_DIM : (head + 1) * HEAD_DIM] = (
            mixed[:, :HEAD_DIM] / row_total
        ).astype(attention_ref.dtype)


def share_of(attention_ref, weight_ref, step, tp_size):
    width = weight_ref.shape[1] // tp_size
    member = lax.rem(lax.axis_index("tp") + step, tp_size)
    columns = pl.ds(pl.multiple_of(member * width, LANES), width)
    return jnp.dot(
        attention_ref[...], weight_ref[:, columns], preferred_element_type=jnp.float32
    )


def project_far(parts, out_weight, heads, groups, rows, step, tp_size):
    features, columns = out_weight.shape

    def body(parts_ref, weight_ref, attention_ref, far_ref):
        combine(parts_ref, attention_ref, heads, groups, rows)
        far_ref[...] = share_of(attention_ref, weight_ref, step, tp_size).astype(far_ref.dtype)

    return pl.pallas_call(
        body,
        out_shape=(
            jax.ShapeDtypeStruct((rows, features), jnp.bfloat16),
            jax.ShapeDtypeStruct((rows, columns // tp_size), jnp.bfloat16),
        ),
        cost_estimate=pl.CostEstimate(
            flops=2 * rows * features * columns // tp_size,
            bytes_accessed=2 * features * columns,
            transcendentals=0,
        ),
        compiler_params=pltpu.CompilerParams(vmem_limit_bytes=VMEM_LIMIT),
    )(parts, out_weight)


def project_near(attention, out_weight, steps, tp_size):
    rows, features = attention.shape
    columns = out_weight.shape[1]

    def body(attention_ref, weight_ref, *out_refs):
        for step, out_ref in zip(steps, out_refs):
            out_ref[...] = share_of(attention_ref, weight_ref, step, tp_size).astype(
                out_ref.dtype
            )

    return pl.pallas_call(
        body,
        out_shape=[
            jax.ShapeDtypeStruct(
                (rows, columns // tp_size), jnp.bfloat16 if step else jnp.float32
            )
            for step in steps
        ],
        cost_estimate=pl.CostEstimate(
            flops=2 * rows * features * len(steps) * (columns // tp_size),
            bytes_accessed=2 * features * columns,
            transcendentals=0,
        ),
        compiler_params=pltpu.CompilerParams(vmem_limit_bytes=VMEM_LIMIT),
    )(attention, out_weight)


def to_member(share, step, tp_size):
    return lax.ppermute(share, "tp", [(i, (i + step) % tp_size) for i in range(tp_size)])


def shards(queries, keys, values, out_weight):
    rows, features = queries.shape
    heads = features // HEAD_DIM
    groups = lax.axis_size("zh")
    key_copies = lax.axis_size("xb") * lax.axis_size("yl") * lax.axis_size("core")
    tp_size = lax.axis_size("tp")

    one_head = lax.all_to_all(
        pack(queries, keys, values, heads), HEAD_AXES, 0, 0, tiled=True
    ).reshape(heads * rows, 3 * LANES)
    own_q, sent_kv = spread(one_head, key_copies)
    got_kv = lax.all_to_all(sent_kv, KEY_AXES, 0, 0, tiled=True)
    got_q = lax.all_gather(own_q, "zh", axis=0, tiled=True)
    partial = attend(got_q, got_kv.reshape(-1, 2 * LANES), rows)
    returned = lax.all_to_all(
        partial.reshape(groups * heads, rows, LANES), RETURN_AXES, 0, 0, tiled=True
    )
    far = tp_size // 2
    near = [step for step in range(1, tp_size) if step != far]
    attention, far_share = project_far(
        returned.reshape(-1, LANES), out_weight, heads, groups, rows, far, tp_size
    )
    arrived = [to_member(far_share, far, tp_size)]
    *near_shares, own_share = project_near(attention, out_weight, near + [0], tp_size)
    arrived += [to_member(share, step, tp_size) for share, step in zip(near_shares, near)]
    total = own_share
    for share in arrived:
        total = total + share.astype(jnp.float32)
    return total.astype(jnp.bfloat16)


def solution(mesh):
    split = Mesh(mesh.devices.reshape(2, 2, 2, 4, 2, 2, 4), AXES)
    placed = (P(CTX, "tp"), P(CTX, "tp"), P(CTX, "tp"), P("tp", None))
    return jax.shard_map(
        shards, mesh=split, in_specs=placed, out_specs=P(CTX, "tp"), check_vma=False
    )
```

```python
import math

import jax
import jax.numpy as jnp
from jax import lax
from jax.experimental import pallas as pl
from jax.experimental.pallas import tpu as pltpu
from jax.sharding import Mesh, PartitionSpec as P

HEAD_DIM = 112
LANES = 128
TOTAL, TOTAL_LOW, SHIFT = HEAD_DIM, HEAD_DIM + 1, HEAD_DIM + 2
NEG_FILL = -1e30
NEG_CLAMP = -1e29
AXES = ("xa", "xb", "yl", "zh", "zl", "core", "tp")
CTX = AXES[:6]
HEAD_AXES = ("xa", "zl")
KEY_AXES = ("xb", "yl", "core")
RETURN_AXES = ("zh",) + HEAD_AXES
VMEM_LIMIT = 48 * 1024 * 1024
EXP2_SCALE = math.log2(math.e) / HEAD_DIM**0.5


def pack(queries, keys, values, heads):
    rows = queries.shape[0]
    kind = queries.dtype

    def body(held, out_ref):
        for head in range(heads):
            columns = slice(head * HEAD_DIM, (head + 1) * HEAD_DIM)
            key, value, query = (
                held[part * rows : (part + 1) * rows, columns] for part in range(3)
            )
            gap = jnp.zeros((rows, LANES - HEAD_DIM), kind)
            out_ref[head] = jnp.concatenate(
                [key, gap, value, jnp.ones_like(gap), query, gap], axis=1
            )

    return pl.pallas_call(
        body,
        out_shape=jax.ShapeDtypeStruct((heads, rows, 3 * LANES), kind),
        compiler_params=pltpu.CompilerParams(vmem_limit_bytes=VMEM_LIMIT),
    )(jnp.concatenate([keys, values, queries], axis=0))


def spread(one_head, copies):
    rows = one_head.shape[0]
    kind = one_head.dtype

    def body(one_ref, q_out, kv_out):
        q_out[...] = one_ref[:, 2 * LANES :]
        pair = one_ref[:, : 2 * LANES]
        for copy in range(copies):
            kv_out[copy] = pair

    return pl.pallas_call(
        body,
        out_shape=(
            jax.ShapeDtypeStruct((rows, LANES), kind),
            jax.ShapeDtypeStruct((copies, rows, 2 * LANES), kind),
        ),
        compiler_params=pltpu.CompilerParams(vmem_limit_bytes=VMEM_LIMIT),
    )(one_head)


def attend_kernel(rows, q_ref, kv_ref, out_ref, key_ref, value_ref):
    xb, yl, zh, core = (lax.axis_index(name) for name in ("xb", "yl", "zh", "core"))
    pair = 2 * rows
    block = 2 * pair
    coarse = 4 * block
    sources = kv_ref.shape[0] // block
    half = sources * pair
    for xa_at in range(2):
        for source in range(sources):
            start = source * block + xa_at * pair
            to_rows = slice(xa_at * half + source * pair, xa_at * half + (source + 1) * pair)
            key_ref[to_rows, :] = kv_ref[start : start + pair, :LANES]
            value_ref[to_rows, :] = kv_ref[start : start + pair, LANES:]
    query_at = lax.broadcasted_iota(jnp.int32, (block, half), 0)
    query_at = (query_at // pair) * block + query_at % pair + (query_at // rows % 2) * rows
    key_at = lax.broadcasted_iota(jnp.int32, (block, half), 1)
    source_at = key_at // pair
    key_at = (
        (source_at // 2) * coarse
        + (source_at % 2) * rows
        + key_at % pair
        + (key_at // rows % 2) * rows
    )
    distance = query_at - key_at + (xb * 2 + yl) * coarse + core * rows - zh * block
    lane = lax.broadcasted_iota(jnp.int32, (block, LANES), 1)
    for zh_at in range(0, q_ref.shape[0] // block, 2):
        kept = distance + zh_at * block >= 0
        for xa_at in range(2):
            total = (xa_at + 1) * half
            known = total - half
            starts = [(zh_at + after) * block + xa_at * pair for after in range(2)]
            queries = jnp.concatenate(
                [q_ref[start : start + pair, :] for start in starts], axis=0
            )
            scores = lax.dot_general(
                queries,
                key_ref[:total, :],
                (((1,), (1,)), ((), ())),
                preferred_element_type=jnp.float32,
            )
            last = jnp.where(kept, scores[:, known:], NEG_FILL)
            if known:
                scores = jnp.concatenate([scores[:, :known], last], axis=1)
            else:
                scores = last
            top = jnp.maximum(jnp.max(scores, axis=1, keepdims=True), NEG_CLAMP)
            shift = (top * EXP2_SCALE).astype(jnp.bfloat16).astype(jnp.float32)
            weights = jnp.exp2(scores * EXP2_SCALE - shift)
            weighted = jnp.dot(
                weights.astype(jnp.bfloat16),
                value_ref[:total, :],
                preferred_element_type=jnp.float32,
            )
            rounded = weighted.astype(jnp.bfloat16).astype(jnp.float32)
            weighted = jnp.where(lane == TOTAL_LOW, weighted - rounded, weighted)
            weighted = jnp.where(lane == SHIFT, shift, weighted).astype(out_ref.dtype)
            for after, start in enumerate(starts):
                out_ref[start : start + pair, :] = weighted[after * pair : (after + 1) * pair]


def attend(queries, keys_values, rows):
    def body(*refs):
        attend_kernel(rows, *refs)

    return pl.pallas_call(
        body,
        out_shape=jax.ShapeDtypeStruct(queries.shape, queries.dtype),
        scratch_shapes=[pltpu.VMEM((keys_values.shape[0], LANES), queries.dtype)] * 2,
        compiler_params=pltpu.CompilerParams(vmem_limit_bytes=VMEM_LIMIT),
    )(queries, keys_values)


def combine(parts_ref, attention_ref, heads, groups, rows):
    for head in range(heads):
        parts = [
            parts_ref[
                (group * heads + head) * rows : (group * heads + head + 1) * rows, :
            ].astype(jnp.float32)
            for group in range(groups)
        ]
        shifts = [part[:, SHIFT : SHIFT + 1] for part in parts]
        top = shifts[0]
        for shift in shifts[1:]:
            top = jnp.maximum(top, shift)
        mixed = jnp.zeros_like(parts[0])
        for shift, part in zip(shifts, parts):
            mixed = mixed + jnp.exp2(shift - top) * part
        row_total = mixed[:, TOTAL : TOTAL + 1] + mixed[:, TOTAL_LOW : TOTAL_LOW + 1]
        attention_ref[:, head * HEAD_DIM : (head + 1) * HEAD_DIM] = (
            mixed[:, :HEAD_DIM] / row_total
        ).astype(attention_ref.dtype)


def project(parts, out_weight, heads, groups, rows, tp_size):
    features, columns = out_weight.shape
    width = columns // tp_size

    def body(parts_ref, weight_ref, out_ref, attention_ref):
        combine(parts_ref, attention_ref, heads, groups, rows)
        for member in range(tp_size):
            out_ref[member] = jnp.dot(
                attention_ref[...],
                weight_ref[:, member * width : (member + 1) * width],
                preferred_element_type=jnp.float32,
            ).astype(out_ref.dtype)

    return pl.pallas_call(
        body,
        out_shape=jax.ShapeDtypeStruct((tp_size, rows, width), jnp.bfloat16),
        scratch_shapes=[pltpu.VMEM((rows, features), jnp.bfloat16)],
        compiler_params=pltpu.CompilerParams(vmem_limit_bytes=VMEM_LIMIT),
    )(parts, out_weight)


def shards(queries, keys, values, out_weight):
    rows, features = queries.shape
    heads = features // HEAD_DIM
    groups = lax.axis_size("zh")
    key_copies = lax.axis_size("xb") * lax.axis_size("yl") * lax.axis_size("core")
    tp_size = lax.axis_size("tp")

    one_head = lax.all_to_all(
        pack(queries, keys, values, heads), HEAD_AXES, 0, 0, tiled=True
    ).reshape(heads * rows, 3 * LANES)
    own_q, sent_kv = spread(one_head, key_copies)
    got_kv = lax.all_to_all(sent_kv, KEY_AXES, 0, 0, tiled=True)
    got_q = lax.all_gather(own_q, "zh", axis=0, tiled=True)
    partial = attend(got_q, got_kv.reshape(-1, 2 * LANES), rows)
    returned = lax.all_to_all(
        partial.reshape(groups * heads, rows, LANES), RETURN_AXES, 0, 0, tiled=True
    )
    shares = project(returned.reshape(-1, LANES), out_weight, heads, groups, rows, tp_size)
    arrived = lax.all_to_all(shares, "tp", 0, 0, tiled=True)
    return jnp.sum(arrived.astype(jnp.float32), axis=0).astype(jnp.bfloat16)


def solution(mesh):
    split = Mesh(mesh.devices.reshape(2, 2, 2, 4, 2, 2, 4), AXES)
    placed = (P(CTX, "tp"), P(CTX, "tp"), P(CTX, "tp"), P("tp", None))
    return jax.shard_map(
        shards, mesh=split, in_specs=placed, out_specs=P(CTX, "tp"), check_vma=False
    )
```

```python
import math

import jax
import jax.numpy as jnp
from jax import lax
from jax.experimental import pallas as pl
from jax.experimental.pallas import tpu as pltpu
from jax.sharding import Mesh, PartitionSpec as P

HEAD_DIM = 112
LANES = 128
TOTAL, TOTAL_LOW, SHIFT = HEAD_DIM, HEAD_DIM + 1, HEAD_DIM + 2
NEG_FILL = -1e30
NEG_CLAMP = -1e29
AXES = ("xa", "xb", "yl", "zh", "zl", "core", "tp")
CTX = AXES[:6]
HEAD_AXES = ("xa", "zl")
KEY_AXES = ("xb", "yl", "core")
RETURN_AXES = ("zh",) + HEAD_AXES
VMEM_LIMIT = 48 * 1024 * 1024
EXP2_SCALE = math.log2(math.e) / HEAD_DIM**0.5


def pack(queries, keys, values, heads):
    rows = queries.shape[0]
    kind = queries.dtype

    def body(held, out_ref):
        for head in range(heads):
            columns = slice(head * HEAD_DIM, (head + 1) * HEAD_DIM)
            key, value, query = (
                held[part * rows : (part + 1) * rows, columns] for part in range(3)
            )
            gap = jnp.zeros((rows, LANES - HEAD_DIM), kind)
            out_ref[head] = jnp.concatenate(
                [key, gap, value, jnp.ones_like(gap), query, gap], axis=1
            )

    return pl.pallas_call(
        body,
        out_shape=jax.ShapeDtypeStruct((heads, rows, 3 * LANES), kind),
        compiler_params=pltpu.CompilerParams(vmem_limit_bytes=VMEM_LIMIT),
    )(jnp.concatenate([keys, values, queries], axis=0))


def spread(one_head, copies):
    rows = one_head.shape[0]
    kind = one_head.dtype

    def body(one_ref, q_out, kv_out):
        q_out[...] = one_ref[:, 2 * LANES :]
        pair = one_ref[:, : 2 * LANES]
        for copy in range(copies):
            kv_out[copy] = pair

    return pl.pallas_call(
        body,
        out_shape=(
            jax.ShapeDtypeStruct((rows, LANES), kind),
            jax.ShapeDtypeStruct((copies, rows, 2 * LANES), kind),
        ),
        compiler_params=pltpu.CompilerParams(vmem_limit_bytes=VMEM_LIMIT),
    )(one_head)


def attend_kernel(rows, q_ref, kv_ref, out_ref, key_ref, value_ref):
    xb, yl, zh, core = (lax.axis_index(name) for name in ("xb", "yl", "zh", "core"))
    pair = 2 * rows
    block = 2 * pair
    coarse = 4 * block
    sources = kv_ref.shape[0] // block
    half = sources * pair
    for xa_at in range(2):
        for source in range(sources):
            start = source * block + xa_at * pair
            to_rows = slice(xa_at * half + source * pair, xa_at * half + (source + 1) * pair)
            key_ref[to_rows, :] = kv_ref[start : start + pair, :LANES]
            value_ref[to_rows, :] = kv_ref[start : start + pair, LANES:]
    query_at = lax.broadcasted_iota(jnp.int32, (block, half), 0)
    query_at = (query_at // pair) * block + query_at % pair + (query_at // rows % 2) * rows
    key_at = lax.broadcasted_iota(jnp.int32, (block, half), 1)
    source_at = key_at // pair
    key_at = (
        (source_at // 2) * coarse
        + (source_at % 2) * rows
        + key_at % pair
        + (key_at // rows % 2) * rows
    )
    distance = query_at - key_at + (xb * 2 + yl) * coarse + core * rows - zh * block
    lane = lax.broadcasted_iota(jnp.int32, (block, LANES), 1)
    for zh_at in range(0, q_ref.shape[0] // block, 2):
        kept = distance + zh_at * block >= 0
        for xa_at in range(2):
            total = (xa_at + 1) * half
            known = total - half
            starts = [(zh_at + after) * block + xa_at * pair for after in range(2)]
            queries = jnp.concatenate(
                [q_ref[start : start + pair, :] for start in starts], axis=0
            )
            scores = lax.dot_general(
                queries,
                key_ref[:total, :],
                (((1,), (1,)), ((), ())),
                preferred_element_type=jnp.float32,
            )
            last = jnp.where(kept, scores[:, known:], NEG_FILL)
            if known:
                scores = jnp.concatenate([scores[:, :known], last], axis=1)
            else:
                scores = last
            top = jnp.maximum(jnp.max(scores, axis=1, keepdims=True), NEG_CLAMP)
            shift = (top * EXP2_SCALE).astype(jnp.bfloat16).astype(jnp.float32)
            weights = jnp.exp2(scores * EXP2_SCALE - shift)
            weighted = jnp.dot(
                weights.astype(jnp.bfloat16),
                value_ref[:total, :],
                preferred_element_type=jnp.float32,
            )
            rounded = weighted.astype(jnp.bfloat16).astype(jnp.float32)
            weighted = jnp.where(lane == TOTAL_LOW, weighted - rounded, weighted)
            weighted = jnp.where(lane == SHIFT, shift, weighted).astype(out_ref.dtype)
            for after, start in enumerate(starts):
                out_ref[start : start + pair, :] = weighted[after * pair : (after + 1) * pair]


def attend(queries, keys_values, rows):
    def body(*refs):
        attend_kernel(rows, *refs)

    return pl.pallas_call(
        body,
        out_shape=jax.ShapeDtypeStruct(queries.shape, queries.dtype),
        scratch_shapes=[pltpu.VMEM((keys_values.shape[0], LANES), queries.dtype)] * 2,
        compiler_params=pltpu.CompilerParams(vmem_limit_bytes=VMEM_LIMIT),
    )(queries, keys_values)


def combine(parts_ref, attention_ref, heads, groups, rows):
    for head in range(heads):
        parts = [
            parts_ref[
                (group * heads + head) * rows : (group * heads + head + 1) * rows, :
            ].astype(jnp.float32)
            for group in range(groups)
        ]
        shifts = [part[:, SHIFT : SHIFT + 1] for part in parts]
        top = shifts[0]
        for shift in shifts[1:]:
            top = jnp.maximum(top, shift)
        mixed = jnp.zeros_like(parts[0])
        for shift, part in zip(shifts, parts):
            mixed = mixed + jnp.exp2(shift - top) * part
        row_total = mixed[:, TOTAL : TOTAL + 1] + mixed[:, TOTAL_LOW : TOTAL_LOW + 1]
        attention_ref[:, head * HEAD_DIM : (head + 1) * HEAD_DIM] = (
            mixed[:, :HEAD_DIM] / row_total
        ).astype(attention_ref.dtype)


def project(parts, out_weight, heads, groups, rows, tp_size):
    features, columns = out_weight.shape
    width = columns // tp_size

    def body(parts_ref, weight_hbm, out_ref, attention_ref, weight_ref, arrived):
        loads = [
            pltpu.make_async_copy(
                weight_hbm.at[:, member * width : (member + 1) * width],
                weight_ref.at[member],
                arrived.at[member],
            )
            for member in range(tp_size)
        ]
        for load in loads:
            load.start()
        combine(parts_ref, attention_ref, heads, groups, rows)
        for member, load in enumerate(loads):
            load.wait()
            out_ref[member] = jnp.dot(
                attention_ref[...], weight_ref[member], preferred_element_type=jnp.float32
            ).astype(out_ref.dtype)

    return pl.pallas_call(
        body,
        in_specs=[pl.BlockSpec(memory_space=pltpu.VMEM), pl.BlockSpec(memory_space=pl.ANY)],
        out_shape=jax.ShapeDtypeStruct((tp_size, rows, width), jnp.bfloat16),
        scratch_shapes=[
            pltpu.VMEM((rows, features), jnp.bfloat16),
            pltpu.VMEM((tp_size, features, width), jnp.bfloat16),
            pltpu.SemaphoreType.DMA((tp_size,)),
        ],
        compiler_params=pltpu.CompilerParams(vmem_limit_bytes=VMEM_LIMIT),
    )(parts, out_weight)


def shards(queries, keys, values, out_weight):
    rows, features = queries.shape
    heads = features // HEAD_DIM
    groups = lax.axis_size("zh")
    key_copies = lax.axis_size("xb") * lax.axis_size("yl") * lax.axis_size("core")
    tp_size = lax.axis_size("tp")

    one_head = lax.all_to_all(
        pack(queries, keys, values, heads), HEAD_AXES, 0, 0, tiled=True
    ).reshape(heads * rows, 3 * LANES)
    own_q, sent_kv = spread(one_head, key_copies)
    got_kv = lax.all_to_all(sent_kv, KEY_AXES, 0, 0, tiled=True)
    got_q = lax.all_gather(own_q, "zh", axis=0, tiled=True)
    partial = attend(got_q, got_kv.reshape(-1, 2 * LANES), rows)
    returned = lax.all_to_all(
        partial.reshape(groups * heads, rows, LANES), RETURN_AXES, 0, 0, tiled=True
    )
    shares = project(returned.reshape(-1, LANES), out_weight, heads, groups, rows, tp_size)
    arrived = lax.all_to_all(shares, "tp", 0, 0, tiled=True)
    return jnp.sum(arrived.astype(jnp.float32), axis=0).astype(jnp.bfloat16)


def solution(mesh):
    split = Mesh(mesh.devices.reshape(2, 2, 2, 4, 2, 2, 4), AXES)
    placed = (P(CTX, "tp"), P(CTX, "tp"), P(CTX, "tp"), P("tp", None))
    return jax.shard_map(
        shards, mesh=split, in_specs=placed, out_specs=P(CTX, "tp"), check_vma=False
    )
```
